128 devices in a mesh: section: 8 (over y, x_hi), expert: 16 (over x_lo, z, core).
Axes of the slice: x: 4 (x_hi: 2, x_lo: 2; x = x_hi * 2 + x_lo), y: 4, z: 4, core: 2. Of those that a mesh axis runs over, the one named last changes fastest.
Arguments:
- kv_grads: bfloat16 [8, 2048, 4096], P('section', 'expert'), may hold values from -6 to 6
- kv_weight: bfloat16 [8, 2048, 4096], P('section', 'expert'), may hold values from -0.09375 to 0.09375
- enc_inputs: bfloat16 [8, 2048, 2048], P('section', 'expert')
- enc_gain: float32 [8, 2048], P('section'), may hold values from 0.25 to 1.75
- enc_w1: bfloat16 [8, 2048, 32768], P('section', None, 'expert'), may hold values from -0.125 to 0.125
- enc_w2: bfloat16 [8, 32768, 2048], P('section', 'expert'), may hold values from -0.0625 to 0.0625
- route_ids: int32 [8, 2048, 2], P('section', 'expert'), may hold values from 0 to 3, all different within a row; in each aligned block of 128 rows (0 to 127, 128 to 255, ..., all dimensions but the last counted through in order) at most 68 rows name the same one
- route_probs: float32 [8, 2048, 2], P('section', 'expert'), may hold values from 0.05 to 0.5
- pending_grads: bfloat16 [8, 2048, 2048], P('section', 'expert'), may hold values from -6 to 6
Outputs:
- section_grads: bfloat16 [8, 2048, 2048], P('section', 'expert')
The draws below stay inside these ranges and needn't reach their ends.
Inputs may be any that keep to these rules, and one draw needn't show every extreme that they name: `route_ids`: within each device's 128 rows (aligned blocks of one section) no expert is chosen more than 68 times, and in some block some expert exactly 68 times; the two choices of a token differ.
All inputs are finite; a program needn't handle non-finite values.
Results may differ from the reference program's by a relative error of at most 0.005.
Values may be sent and summed in bfloat16 or wider, within the bound.
A program may use at most 128 MiB of HBM per device.

```python
import math
from functools import partial
import jax
import jax.numpy as jnp
import numpy as np
from jax import lax

D = 2048
FF = 8192
EXPERTS = 4
TOK_DEV = 128
CAP = 68
SHARDS = 4
TOKENS = 2048
N_SECTION = 8


def draw_enc_inputs(key, part):
    key = jax.random.fold_in(key, 7)
    keys = jax.random.split(key, 3)
    shape = (N_SECTION, TOKENS, D)
    base = jax.random.normal(keys[0], shape, jnp.float32)
    row_scale = jnp.exp(jax.random.uniform(keys[1], (N_SECTION, TOKENS, 1), jnp.float32, math.log(0.25), math.log(2.5)))
    column_norm = math.sqrt(99.0 / (2.0 * math.log(10.0)))
    column_scale = jnp.exp(jax.random.uniform(keys[2], (N_SECTION, 1, D), jnp.float32, 0.0, math.log(10.0))) / column_norm
    return (base * row_scale * column_scale).astype(jnp.bfloat16)


def level_of(own_key, shape, cuts, low, top_value):
    def one(axis_at, parts):
        draws = jax.random.uniform(jax.random.fold_in(jax.random.fold_in(own_key, 6), axis_at), (parts,), jnp.float32, low / len(cuts), top_value / len(cuts))
        return jnp.repeat(jnp.exp(draws), shape[axis_at] // parts).reshape((-1,) + (1,) * (len(shape) - axis_at - 1))

    level = one(*cuts[0])
    for cut in cuts[1:]:
        level = level * one(*cut)
    return level


def routed_block(own_key, own, number, rows, amount, top, bound, slope):
    order = jax.random.permutation(own_key, amount)
    packed, ordinary = shares(amount, rows * top, bound, slope, True), shares(amount, rows * top, bound, slope, False)
    places = jnp.arange(amount)

    def named(sizes, turn):
        used = int((sizes > 0).sum())
        fixed = max(1, used // 4)
        shifted = fixed + (places - fixed + turn * (used - fixed)) % max(1, amount - fixed)
        return jnp.zeros((amount,), jnp.int32).at[order[jnp.where(places < fixed, places, shifted)]].set(jnp.asarray(sizes, jnp.int32))

    sizes = jnp.where(number % 4 == 0, named(packed, number // 4), named(ordinary, number - number // 4 - 1))
    mixed = jax.random.permutation(jax.random.fold_in(own, 3), amount)
    donor, sink = mixed[0:amount // 2 * 2:2], mixed[1:amount // 2 * 2:2]
    slack = jnp.minimum(sizes[donor] - 1, bound - sizes[sink]) // 2
    slack = jnp.where((donor == order[0]) | (sink == order[0]) | (sizes[sink] == 0), 0, jnp.maximum(slack, 0))
    shifted = jax.random.randint(jax.random.fold_in(own, 4), (amount // 2,), 0, 1 << 20) % (slack + 1)
    sizes = sizes.at[donor].add(-shifted).at[sink].add(shifted)
    members = jnp.searchsorted(jnp.cumsum(sizes), jnp.arange(rows * top), side="right").astype(jnp.int32)
    grid = members.reshape(top, rows).T
    grid = grid[jax.random.permutation(jax.random.fold_in(own, 1), rows)]
    turn = jax.random.randint(jax.random.fold_in(own, 2), (rows, 1), 0, top)
    return jnp.take_along_axis(grid, (jnp.arange(top)[None, :] + turn) % top, axis=1)


def shares(number_of, total, reach, lean, full):
    portions = [(1 << 20) // math.isqrt(rank ** lean) + 1 for rank in range(1, number_of + 1)]
    largest = reach if full else min(reach, max(-(-total // number_of), total * portions[0] // sum(portions)))
    least = 1 if total - largest >= number_of - 1 else 0
    given, surplus = [largest] + [least] * (number_of - 1), total - largest - least * (number_of - 1)
    while surplus > 0:
        candidates = [i for i in range(1, number_of) if given[i] < largest] or [i for i in range(1, number_of) if given[i] < reach]
        mass, left = sum([portions[i] for i in candidates]), surplus
        for i in candidates:
            extra = min(reach - given[i], max(1, left * portions[i] // mass), surplus)
            given[i] = given[i] + extra
            surplus = surplus - extra
    return np.array(given)


def bell_draw(own_key, dims, scale, limit, cuts=(), kind=jnp.bfloat16):
    drawn = jax.random.normal(own_key, dims, jnp.float32) * scale
    if len(cuts) > 0:
        drawn = level_of(own_key, dims, cuts, -0.22, 0.18) * drawn
    return jnp.clip(drawn, min=-limit, max=limit).astype(kind)


def setup_inputs(seed: int = 0) -> dict:
    seeds = jax.random.split(jax.random.key(seed), 10)
    kv_grads = bell_draw(seeds[0], (N_SECTION, TOKENS, 2 * D), 1.0, 6.0, ((0, 8), (1, 16)))
    kv_weight = bell_draw(seeds[1], (N_SECTION, D, 2 * D), (2 * D) ** -0.5, 0.09375, ((0, 8), (1, 16)))
    enc_inputs = draw_enc_inputs(jax.random.fold_in(seeds[9], 71), 0)
    enc_gain = jnp.clip(1.0 + 0.15 * jax.random.normal(seeds[3], (N_SECTION, D), jnp.float32), 0.25, 1.75)
    enc_w1 = bell_draw(seeds[4], (N_SECTION, D, EXPERTS * FF), D ** -0.5, 0.125, ((0, 8), (2, 16)))
    enc_w2 = bell_draw(seeds[5], (N_SECTION, EXPERTS * FF, D), FF ** -0.5, 0.0625, ((0, 8), (1, 16)))
    route_ids_keys = jax.random.split(jax.random.fold_in(seeds[6], 1), N_SECTION * TOKENS // TOK_DEV)
    route_ids_turns = jax.random.permutation(jax.random.fold_in(seeds[6], 3), N_SECTION * TOKENS // TOK_DEV)
    route_ids = jax.vmap(lambda own, number: routed_block(jax.random.fold_in(seeds[6], 2), own, number, TOK_DEV, EXPERTS, 2, CAP, 1))(route_ids_keys, route_ids_turns).reshape((N_SECTION, TOKENS, 2))
    route_probs = jnp.clip(jnp.exp(math.log(0.5) - 2.3025851 * jax.random.uniform(seeds[7], (N_SECTION, TOKENS, 2), jnp.float32) ** level_of(seeds[7], (N_SECTION, TOKENS, 2), ((0, 8), (1, 16)), -0.2, 0.2)), 0.05, 0.5)
    pending_grads = bell_draw(seeds[8], (N_SECTION, TOKENS, D), 1.0, 6.0, ((0, 8), (1, 16)))
    return dict(kv_grads=kv_grads, kv_weight=kv_weight, enc_inputs=enc_inputs, enc_gain=enc_gain, enc_w1=enc_w1, enc_w2=enc_w2, route_ids=route_ids, route_probs=route_probs, pending_grads=pending_grads)


EPSILON = 1e-06

def rms_map(inputs, gain):
    values = inputs.astype(jnp.float32)
    factor = lax.rsqrt(lax.optimization_barrier(jnp.mean(values * values, axis=-1, keepdims=True)) + EPSILON)
    return values * factor * gain

def gelu_back(pre_act, upstream):
    return jax.vjp(partial(jax.nn.gelu, approximate=True), pre_act)[1](upstream)[0]

def contract_last(left_side, right_side):
    return lax.dot_general(left_side, right_side, (((1,), (1,)), ((), ())), preferred_element_type=jnp.float32)

def slot_positions(expert_ids, experts, capacity):
    flat_ids = expert_ids.reshape(-1)
    one_hot = (flat_ids[:, None] == jnp.arange(experts, dtype=jnp.int32)[None, :]).astype(jnp.int32)
    earlier = jnp.cumsum(one_hot, axis=0) - one_hot
    within = lax.optimization_barrier(jnp.sum(earlier * one_hot, axis=1))
    return (flat_ids * capacity + within).reshape(expert_ids.shape).astype(jnp.int32)

def dispatch(positions, first_rows, second_rows, places):
    slot_ids = jnp.arange(places, dtype=jnp.int32)[:, None]
    first_hot = (slot_ids == positions[None, :, 0]).astype(jnp.bfloat16)
    second_hot = (slot_ids == positions[None, :, 1]).astype(jnp.bfloat16)
    summed = jnp.dot(first_hot, first_rows, preferred_element_type=jnp.float32)
    summed = summed + jnp.dot(second_hot, second_rows, preferred_element_type=jnp.float32)
    return summed.astype(jnp.bfloat16)

def section_back(inputs, gain, weight_in, weight_out, expert_ids, probs, incoming):
    width = inputs.shape[1]
    blocks = inputs.shape[0] // TOK_DEV
    places = EXPERTS * CAP
    normed = rms_map(inputs, gain).astype(jnp.bfloat16)
    upper_f = incoming.astype(jnp.float32)
    scaled_first = (probs[:, 0:1] * upper_f).astype(jnp.bfloat16)
    scaled_second = (probs[:, 1:2] * upper_f).astype(jnp.bfloat16)
    positions = jax.vmap(lambda block_ids: slot_positions(block_ids, EXPERTS, CAP))(expert_ids.reshape(blocks, TOK_DEV, 2))

    def block_slots(pieces):
        block_pos, block_normed, block_first, block_second = pieces
        return (dispatch(block_pos, block_normed, block_normed, places), dispatch(block_pos, block_first, block_second, places))
    normed_slots, scaled_slots = lax.map(block_slots, (positions, normed.reshape(blocks, TOK_DEV, width), scaled_first.reshape(blocks, TOK_DEV, width), scaled_second.reshape(blocks, TOK_DEV, width)))
    normed_slots = normed_slots.reshape(blocks, EXPERTS, CAP, width)
    scaled_slots = scaled_slots.reshape(blocks, EXPERTS, CAP, width)
    shard_width = FF // SHARDS
    expert_backs = []
    for expert in range(EXPERTS):
        normed_rows = normed_slots[:, expert].reshape(-1, width)
        scaled_rows = scaled_slots[:, expert].reshape(-1, width)
        summed = jnp.zeros(normed_rows.shape, jnp.float32)
        for shard in range(SHARDS):
            start = expert * FF + shard * shard_width
            in_block = weight_in[:, start:start + shard_width]
            out_block = weight_out[start:start + shard_width, :]
            pre_act = jnp.dot(normed_rows, in_block, preferred_element_type=jnp.float32)
            upstream = contract_last(scaled_rows, out_block)
            hidden_grad = gelu_back(pre_act, upstream).astype(jnp.bfloat16)
            piece = contract_last(hidden_grad, in_block).astype(jnp.bfloat16)
            summed = summed + lax.optimization_barrier(piece).astype(jnp.float32)
        expert_backs.append(summed.reshape(blocks, CAP, width))
    combined = jnp.stack(expert_backs, axis=1).reshape(blocks, places, width)

    def pick(block_back, block_pos):
        return block_back[block_pos[:, 0]] + block_back[block_pos[:, 1]]
    normed_grad = jax.vmap(pick)(combined, positions).reshape(-1, width)
    back_fn = jax.vjp(lambda inner: rms_map(inner, gain), inputs.astype(jnp.float32))[1]
    return (upper_f + back_fn(normed_grad)[0]).astype(jnp.bfloat16)

def reference(kv_grads, kv_weight, enc_inputs, enc_gain, enc_w1, enc_w2, route_ids, route_probs, pending_grads):
    sections = kv_grads.shape[0]
    memory_grad = jnp.zeros((kv_grads.shape[1], kv_weight.shape[1]), jnp.float32)
    for section in range(sections):
        memory_grad = memory_grad + contract_last(kv_grads[section], kv_weight[section])
    memory_rounded = memory_grad.astype(jnp.bfloat16)
    results = []
    for section in range(sections):
        if section == sections - 1:
            incoming = memory_rounded
        else:
            incoming = pending_grads[section + 1]
        results.append(section_back(enc_inputs[section], enc_gain[section], enc_w1[section], enc_w2[section], route_ids[section], route_probs[section], incoming))
    return jnp.stack(results)
```

```python
from functools import partial

import jax
import jax.numpy as jnp
from jax import lax
from jax.experimental import pallas as pl
from jax.experimental.pallas import tpu as pltpu
from jax.sharding import PartitionSpec as P

EXPERTS = 4
CAP = 68
EPSILON = 1e-06

TOK = 128
D = 2048
HALF = D // 2
BLOCK = 144
SIDE = EXPERTS * BLOCK
STEP = 256
LANES = 4
QUARTER = 1024
PLANE = LANES * TOK
CHUNK = 32
PEERS = 16
SECTIONS = 8
BF = jnp.bfloat16
F32 = jnp.float32
MESH = pl.DeviceIdType.MESH


def rms_map(inputs, gain):
    values = inputs.astype(F32)
    factor = lax.rsqrt(jnp.mean(values * values, axis=-1, keepdims=True) + EPSILON)
    return values * factor * gain


def gelu_slope(x):
    scale = 0.7978845608028654
    square = x * x
    t = jnp.tanh(scale * x * (1.0 + 0.044715 * square))
    return 0.5 * (1.0 + t) + 0.5 * x * (1.0 - t * t) * (scale * (1.0 + 3 * 0.044715 * square))


def dot_nt(left, right):
    return lax.dot_general(left, right, (((1,), (1,)), ((), ())), preferred_element_type=F32)


def dot_nn(left, right):
    return jnp.dot(left, right, preferred_element_type=F32)


def rows_of(block):
    return pl.ds(block * BLOCK, BLOCK)


def tick_kernel(
    kvg, kvw, pend, normed, wmat, stmat, w1, w2,
    ng, inc_out,
    W1, W2, GA, GB, QS, QR, QO, PF, RS, FIN, INC, INCX, TK, WX, STX, LN, LS, XN, XS,
    GP, PH, SB, SR, PS, PR, CS, CR, NS, NR,
    loc, ex_s, ex_r, pe_s, inc_r, kv_s, kv_r, zk_s, zk_r, q_s, q_r, rs_s, rs_r, fi_s, ix_s, ix_r,
    st_s, st_r, pa_s, pa_r, sb_s, sb_r, ss_s, ss_r, ps_s, ps_r, cr_s, cr_r, n_s, n_r,
):
    s = lax.axis_index("section")
    e = lax.axis_index("expert")
    xl, z, c = e // 8, (e // 2) % 4, e % 2
    oc, ox = 1 - c, 1 - xl
    zi = z + 1 - 2 * (z % 2)
    zc = 3 - z
    me = s * 2 + xl
    lane = xl * 2 + c

    def dev(x, zz, cc, sec=s):
        return (sec, x * 8 + zz * 2 + cc)

    sib, partner, crossed = dev(xl, z, oc), dev(xl, zi, c), dev(xl, zc, c)
    lanes = [(xl, c), (xl, oc), (ox, c), (ox, oc)]
    group = [None, dev(ox, z, c), dev(xl, zc, c), dev(ox, zc, c)]

    def rc(src, dst, send, recv, where):
        return pltpu.make_async_remote_copy(
            src_ref=src, dst_ref=dst, send_sem=send, recv_sem=recv, device_id=where, device_id_type=MESH
        )

    barrier = pltpu.get_barrier_semaphore()

    def greet(where):
        pl.semaphore_signal(barrier, inc=1, device_id=where, device_id_type=MESH)

    for where in (sib, dev(ox, z, c), dev(ox, z, oc), partner, crossed, dev(ox, zc, c)):
        greet(where)

    def greet_peer(i, _):
        k = (me + i) % PEERS
        greet(dev(k % 2, z, c, k // 2))
        return 0

    lax.fori_loop(1, PEERS, greet_peer, 0)

    @pl.when(s < SECTIONS - 1)
    def _():
        greet(dev(xl, z, 0, s + 1))
        greet(dev(xl, z, 1, s + 1))

    @pl.when(s == SECTIONS - 1)
    def _():
        def greet_source(i, _):
            k = xl * 8 + i

            @pl.when(jnp.logical_not((k == me) & (c == 0)))
            def _():
                greet(dev(k % 2, z, 0, k // 2))

            greet(dev(k % 2, zi, 1, k // 2))
            return 0

        lax.fori_loop(0, PEERS // 2, greet_source, 0)

    zt = z + c * (zi - z)
    lane_t = me // 4
    xt, ct, sub = lane_t // 2, lane_t % 2, me % 4
    own_final = (s == SECTIONS - 1) & (xt == xl) & (zt == z)
    to_self = own_final.astype(jnp.int32)
    pl.semaphore_wait(barrier, 6 + PEERS - 1 + 2 * (s > 0).astype(jnp.int32) + 2 - to_self)

    sends = []

    def lane_rows(x, cc):
        return pl.ds(pl.multiple_of((x * 2 + cc) * TOK, TOK), TOK)

    def lane_cols(x, cc):
        return pl.ds(pl.multiple_of((x * 2 + cc) * QUARTER, QUARTER), QUARTER)

    mine = lane_rows(xl, c)
    kv = []
    for r in range(LANES):
        pair = []
        for i, (source, held) in enumerate(((kvg, GA), (kvw, GB))):
            x, cc = lanes[r]
            part = source.at[:, lane_cols(x, cc)]
            if r == 0:
                pair.append(pltpu.make_async_copy(part, held.at[0, mine], loc.at[i]))
            else:
                pair.append(rc(part, held.at[0, mine], kv_s.at[i, r], kv_r.at[i, r], dev(x, z, cc)))
        kv.append(pair)

    def z_copy(i, r):
        held, where = (GA, partner) if i == 0 else (GB, crossed)
        x, cc = lanes[r]
        rows = lane_rows(x, cc)
        if r == 0:
            source = (kvg, kvw)[i].at[:, lane_cols(xl, c)]
        else:
            source = held.at[0, rows]
        return rc(source, held.at[1, rows], zk_s.at[i, r], zk_r.at[i, r], where)

    zk = [[z_copy(i, r) for i in range(2)] for r in range(LANES)]

    exchange = [
        rc(normed.at[:, pl.ds(pl.multiple_of(oc * HALF, HALF), HALF)],
           TK.at[pl.ds(pl.multiple_of(c * TOK, TOK), TOK)], ex_s.at[0], ex_r.at[0], sib),
        rc(wmat, WX.at[c], ex_s.at[1], ex_r.at[1], sib),
        rc(stmat, STX.at[c], ex_s.at[2], ex_r.at[2], sib),
    ]
    for copy in exchange:
        copy.start()
    for r in (2, 3, 1):
        kv[r][0].start()
        kv[r][1].start()
    for i in range(2):
        zk[0][i].start()
    for i in range(2):
        kv[0][i].start()

    def pend_copy(core):
        return rc(pend.at[:, pl.ds(core * HALF, HALF)], INC.at[pl.ds(pl.multiple_of(c * TOK, TOK), TOK)],
                  pe_s.at[core], inc_r, dev(xl, z, core, s - 1))

    @pl.when(s > 0)
    def _():
        pend_copy(0).start()
        pend_copy(1).start()

    load1 = pltpu.make_async_copy(w1, W1, loc.at[2])
    load2 = pltpu.make_async_copy(w2, W2, loc.at[3])
    load1.start()
    load2.start()

    my_cols = pl.ds(pl.multiple_of(c * HALF, HALF), HALF)
    their_cols = pl.ds(pl.multiple_of(oc * HALF, HALF), HALF)
    my_toks = pl.ds(pl.multiple_of(c * TOK, TOK), TOK)
    their_toks = pl.ds(pl.multiple_of(oc * TOK, TOK), TOK)

    TK[my_toks, :] = normed[:, my_cols]
    WX[c] = wmat[...]
    STX[c] = stmat[...]
    for copy in exchange:
        copy.wait_recv()

    def weights_of(r):
        both = jnp.concatenate([WX[0, rows_of(r), :], WX[1, rows_of(r), :]], axis=1)
        return both, (both > 0).astype(BF)

    def stage1(a, r):
        out, held = ((LN, XN), (LS, XS))[a]
        return rc(out.at[r], held.at[0, c, rows_of(r)], st_s.at[a, r], st_r.at[a, r], group[r])

    def to_partner(a, r):
        held = (XN, XS)[a]
        return rc(held.at[0, c, rows_of(r)], held.at[1, c, rows_of(r)], pa_s.at[a, r], pa_r.at[a, r], partner)

    def to_sib(a, h, r):
        block = (XN, XS)[a].at[h, c, rows_of(r)]
        return rc(block, block, sb_s.at[a, h, r], sb_r.at[a, h, r], sib)

    def from_sib(a, h, r):
        block = (XN, XS)[a].at[h, oc, rows_of(r)]
        return rc(block, block, sb_s.at[a, h, r], sb_r.at[a, h, r], sib)

    def go(copy):
        copy.start()
        sends.append(copy)

    def forward(a, r):
        stage1(a, r).wait_recv()
        go(to_partner(a, r))
        go(to_sib(a, 0, r))

    def hand_over(a, r):
        to_partner(a, r).wait_recv()
        go(to_sib(a, 1, r))

    def take(a, h, blocks):
        for r in blocks:
            from_sib(a, h, r).wait_recv()

    for r in (0, 1, 2, 3):
        _, hot = weights_of(r)
        slots = dot_nn(hot, TK[...]).astype(BF)
        if r == 0:
            XN[0, c, rows_of(0)] = slots
            go(to_partner(0, 0))
            go(to_sib(0, 0, 0))
        else:
            LN[r] = slots
            go(stage1(0, r))

    for r in (1, 2, 3):
        for i in range(2):
            kv[r][i].wait_recv()
            zk[r][i].start()
    forward(0, 1)
    forward(0, 2)
    for i in range(2):
        kv[0][i].wait()
    for r in range(LANES):
        for i in range(2):
            zk[r][i].wait_recv()

    def product(plane, store):
        def tile(j, _):
            cols = pl.ds(pl.multiple_of(j * STEP, STEP), STEP)
            for other in range(2):
                store(other, j, dot_nt(GA[plane], GB[other, cols, :]))
            return 0

        lax.fori_loop(0, PLANE // STEP, tile, 0)

    def keep_theirs(other, j, value):
        QS[:, pl.ds(pl.multiple_of(other * PLANE + j * STEP, STEP), STEP)] = value.astype(BF)

    def keep_mine(other, j, value):
        PF[:, pl.ds(pl.multiple_of(other * PLANE + j * STEP, STEP), STEP)] = value

    product(oc, keep_theirs)
    swap = rc(QS, QR, q_s, q_r, sib)
    swap.start()
    product(c, keep_mine)
    forward(0, 3)
    swap.wait_recv()

    def add_core(j, _):
        rows = pl.ds(pl.multiple_of(j * 64, 64), 64)
        QO[rows, :] = (PF[rows, :] + QR[rows, :].astype(F32)).astype(BF)
        return 0

    lax.fori_loop(0, PLANE // 64, add_core, 0)

    def share(k):
        rows = pl.ds(pl.multiple_of(k * CHUNK, CHUNK), CHUNK)
        return rc(QO.at[rows], RS.at[me], rs_s.at[k], rs_r.at[me], dev(k % 2, z, c, k // 2))

    def share_in(k):
        return rc(RS.at[k], RS.at[k], rs_s.at[k], rs_r.at[k], dev(k % 2, z, c, k // 2))

    def send_share(i, _):
        share((me + i) % PEERS).start()
        return 0

    lax.fori_loop(1, PEERS, send_share, 0)
    RS[me] = QO[pl.ds(pl.multiple_of(me * CHUNK, CHUNK), CHUNK), :]

    def pre_act(h, first, last):
        def tile(j, _):
            cols = pl.ds(pl.multiple_of(j * STEP, STEP), STEP)
            total = dot_nn(XN[h, 0], W1[pl.ds(0, HALF), cols]) + dot_nn(XN[h, 1], W1[pl.ds(HALF, HALF), cols])
            GP[h, :, cols] = gelu_slope(total).astype(BF)
            return 0

        lax.fori_loop(first, last, tile, 0)

    load1.wait()
    hand_over(0, 0)
    hand_over(0, 1)
    take(0, 0, range(4))
    pre_act(0, 0, 8)
    hand_over(0, 2)

    def wait_share(i, _):
        share_in((me + i) % PEERS).wait_recv()
        return 0

    lax.fori_loop(1, PEERS, wait_share, 0)
    total = RS[0].astype(F32)
    for k in range(1, PEERS):
        total = total + RS[k].astype(F32)
    FIN[...] = total.astype(BF)

    def final(p, x, op):
        zz = z if p == 0 else zc
        source = FIN.at[:, pl.ds(p * PLANE + x * STEP, STEP)]
        rows = pl.ds(pl.multiple_of(ct * TOK + sub * CHUNK, CHUNK), CHUNK)
        place = INC.at[rows, pl.ds(pl.multiple_of(zz * STEP, STEP), STEP)]
        away = rc(source, place, fi_s.at[p, x], inc_r, dev(xt, zt, x, SECTIONS - 1))
        at_home = jnp.logical_and(own_final, c == x)

        @pl.when(jnp.logical_not(at_home))
        def _():
            away.start() if op == "start" else away.wait_send()

        if op == "start":
            @pl.when(at_home)
            def _():
                pltpu.make_async_copy(source, place, inc_r).start()

    for p in range(2):
        for x in range(2):
            final(p, x, "start")
    hand_over(0, 3)
    take(0, 1, range(4))
    pre_act(1, 0, 3)
    pltpu.make_async_copy(INC, INC, inc_r).wait()

    inc_swap = rc(INC.at[their_toks], INCX, ix_s, ix_r, sib)
    for r in (0, 1, 2, 3):
        both, hot = weights_of(r)
        slots = (dot_nn(hot, INC[...]) * jnp.sum(both, axis=1, keepdims=True)).astype(BF)
        if r == 0:
            XS[0, c, rows_of(0)] = slots
            go(to_partner(1, 0))
            go(to_sib(1, 0, 0))
        else:
            LS[r] = slots
            go(stage1(1, r))
    go(inc_swap)
    pre_act(1, 3, 6)
    forward(1, 1)
    forward(1, 2)
    hand_over(1, 0)
    pre_act(1, 6, 8)
    forward(1, 3)
    load2.wait()

    def hidden(h, first, rows):
        span = pl.ds(first, rows)

        def tile(j, _):
            cols = pl.ds(pl.multiple_of(j * STEP, STEP), STEP)
            upstream = dot_nt(XS[h, 0, span], W2[cols, pl.ds(0, HALF)]) + dot_nt(XS[h, 1, span], W2[cols, pl.ds(HALF, HALF)])
            GP[h, span, cols] = (upstream * GP[h, span, cols].astype(F32)).astype(BF)
            return 0

        lax.fori_loop(0, D // STEP, tile, 0)

    def pieces(h, first, rows):
        span = pl.ds(first, rows)
        for core, kept in ((oc, SB), (c, PH)):
            def tile(j, _, core=core, kept=kept):
                wide = pl.ds(pl.multiple_of(core * HALF + j * STEP, STEP), STEP)
                cols = pl.ds(pl.multiple_of(j * STEP, STEP), STEP)
                kept[h, span, cols] = dot_nt(GP[h, span, :], W1[wide, :]).astype(BF)
                return 0

            lax.fori_loop(0, HALF // STEP, tile, 0)
            if kept is SB:
                go(core_sum(h, first, rows))

    def core_sum(h, first, rows):
        span = pl.ds(first, rows)
        i = 2 * h + first // (2 * BLOCK)
        return rc(SB.at[h, span], SR.at[h, span], ss_s.at[i], ss_r.at[i], sib)

    def partner_sum(i):
        span = pl.ds(i * 2 * BLOCK, 2 * BLOCK)
        return rc(PS.at[span], PR.at[span], ps_s.at[i], ps_r.at[i], partner)

    def add_cores(i):
        core_sum(1, i * 2 * BLOCK, 2 * BLOCK).wait_recv()

        def some(j, _):
            rows = pl.ds(pl.multiple_of(i * 2 * BLOCK + j * 48, 16), 48)
            PS[rows, :] = (PH[1, rows, :].astype(F32) + SR[1, rows, :].astype(F32)).astype(BF)
            return 0

        lax.fori_loop(0, 6, some, 0)
        go(partner_sum(i))

    take(1, 0, range(4))
    hidden(0, 0, SIDE)
    hand_over(1, 1)
    pieces(0, 0, SIDE)
    hand_over(1, 2)
    take(1, 1, (0, 1))
    hidden(1, 0, 2 * BLOCK)
    pieces(1, 0, 2 * BLOCK)
    hand_over(1, 3)
    add_cores(0)
    take(1, 1, (2, 3))
    hidden(1, 2 * BLOCK, 2 * BLOCK)
    pieces(1, 2 * BLOCK, 2 * BLOCK)
    add_cores(1)

    def give_back(r):
        return rc(CS.at[r], CR.at[r], cr_s.at[r], cr_r.at[r], group[r])

    core_sum(0, 0, SIDE).wait_recv()
    for r in (0, 1, 2, 3):
        if r % 2 == 0:
            partner_sum(r // 2).wait_recv()
        held = CR if r == 0 else CS

        def some(j, _, r=r, held=held):
            rows = pl.ds(pl.multiple_of(r * BLOCK + j * 48, 16), 48)
            value = PH[0, rows, :].astype(F32) + SR[0, rows, :].astype(F32) + PR[rows, :].astype(F32)
            held[r, pl.ds(pl.multiple_of(j * 48, 16), 48), :] = value.astype(BF)
            return 0

        lax.fori_loop(0, 3, some, 0)
        if r > 0:
            go(give_back(r))
    for r in (1, 2, 3):
        give_back(r).wait_recv()

    def gathered(core):
        total = dot_nn(STX[core, :, pl.ds(0, BLOCK)], CR[0])
        for r in range(1, EXPERTS):
            total = total + dot_nn(STX[core, :, pl.ds(r * STEP, BLOCK)], CR[r])
        return total

    NS[...] = gathered(oc)
    last = rc(NS, NR, n_s, n_r, sib)
    go(last)
    ng[:, my_cols] = gathered(c)
    inc_out[:, my_cols] = INC[my_toks, :]
    inc_swap.wait_recv()
    inc_out[:, their_cols] = INCX[...]
    last.wait_recv()
    ng[:, their_cols] = NR[...]

    for copy in exchange:
        copy.wait_send()
    for r in range(LANES):
        for i in range(2):
            if r > 0:
                kv[r][i].wait_send()
            zk[r][i].wait_send()

    @pl.when(s > 0)
    def _():
        pend_copy(0).wait_send()
        pend_copy(1).wait_send()

    swap.wait_send()

    def sent_share(i, _):
        share((me + i) % PEERS).wait_send()
        return 0

    lax.fori_loop(1, PEERS, sent_share, 0)
    for p in range(2):
        for x in range(2):
            final(p, x, "wait")
    for copy in sends:
        copy.wait_send()


def tick(kvg, kvw, pend, normed, wmat, stmat, w1, w2):
    any_place = pl.BlockSpec(memory_space=pl.ANY)
    vmem = pl.BlockSpec(memory_space=pltpu.VMEM)
    dma = pltpu.SemaphoreType.DMA
    V = pltpu.VMEM
    scratch = [
        V((D, D), BF), V((D, D), BF),
        V((2, PLANE, QUARTER), BF), V((2, PLANE, QUARTER), BF),
        V((PLANE, HALF), BF), V((PLANE, HALF), BF), V((PLANE, HALF), BF), V((PLANE, HALF), F32),
        V((PEERS, CHUNK, HALF), BF), V((CHUNK, HALF), BF),
        V((2 * TOK, HALF), BF), V((TOK, HALF), BF), V((2 * TOK, HALF), BF),
        V((2, SIDE, TOK), F32), V((2, TOK, EXPERTS * STEP), BF),
        V((EXPERTS, BLOCK, HALF), BF), V((EXPERTS, BLOCK, HALF), BF),
        V((2, 2, SIDE, HALF), BF), V((2, 2, SIDE, HALF), BF),
        V((2, SIDE, D), BF),
        V((2, SIDE, HALF), BF), V((2, SIDE, HALF), BF), V((2, SIDE, HALF), BF),
        V((SIDE, HALF), BF), V((SIDE, HALF), BF),
        V((EXPERTS, BLOCK, HALF), BF), V((EXPERTS, BLOCK, HALF), BF),
        V((TOK, HALF), F32), V((TOK, HALF), F32),
        dma((4,)), dma((3,)), dma((3,)), dma((2,)), dma, dma((2, 4)), dma((2, 4)), dma((2, 4)), dma((2, 4)),
        dma, dma, dma((PEERS,)), dma((PEERS,)), dma((2, 2)), dma, dma,
        dma((2, 4)), dma((2, 4)), dma((2, 4)), dma((2, 4)), dma((2, 2, 4)), dma((2, 2, 4)),
        dma((4,)), dma((4,)), dma((2,)), dma((2,)), dma((4,)), dma((4,)), dma, dma,
    ]
    return pl.pallas_call(
        tick_kernel,
        out_shape=(jax.ShapeDtypeStruct((TOK, D), F32), jax.ShapeDtypeStruct((TOK, D), BF)),
        in_specs=[any_place] * 3 + [vmem] * 3 + [any_place] * 2,
        out_specs=(vmem, vmem),
        scratch_shapes=scratch,
        compiler_params=pltpu.CompilerParams(
            collective_id=0, has_side_effects=True, vmem_limit_bytes=62 * 1024 * 1024
        ),
        name="tick",
    )(kvg, kvw, pend, normed, wmat, stmat, w1, w2)


def routes(ids, probs):
    e = lax.axis_index("expert")
    xl, zh, c = e // 8, (e // 4) % 2, e % 2
    block = (ids // 2 != xl).astype(jnp.int32) + 2 * (ids % 2 != zh).astype(jnp.int32)
    used = (block[:, :, None] == jnp.arange(EXPERTS)[None, None, :]).any(axis=1)
    order = jnp.arange(TOK)
    earlier = (order[None, :] < order[:, None]).astype(BF)
    ahead = dot_nn(earlier, used.astype(BF)).astype(jnp.int32)
    within = jnp.take_along_axis(ahead, block, axis=1) + c * CAP
    slot = block * BLOCK + within
    place = jnp.arange(SIDE)[:, None]
    wmat = jnp.where(place == slot[None, :, 0], probs[None, :, 0], 0.0)
    wmat = wmat + jnp.where(place == slot[None, :, 1], probs[None, :, 1], 0.0)
    wide = block * STEP + within
    column = jnp.arange(EXPERTS * STEP)[None, :]
    stmat = ((column == wide[:, 0:1]) | (column == wide[:, 1:2])).astype(BF)
    return wmat, stmat


def body(
    kv_grads, kv_weight, enc_inputs, enc_gain, enc_w1, enc_w2, route_ids, route_probs, pending_grads
):
    normed = rms_map(enc_inputs[0], enc_gain[0]).astype(BF)
    wmat, stmat = routes(route_ids[0], route_probs[0])
    normed_grad, incoming = tick(
        kv_grads[0], kv_weight[0], pending_grads[0], normed, wmat, stmat, enc_w1[0], enc_w2[0]
    )
    back_fn = jax.vjp(lambda inner: rms_map(inner, enc_gain[0]), enc_inputs[0].astype(F32))[1]
    result = (incoming.astype(F32) + back_fn(normed_grad)[0]).astype(BF)
    return result[None]


def solution(mesh):
    return jax.shard_map(
        body,
        mesh=mesh,
        in_specs=(
            P("section", "expert", None),
            P("section", "expert", None),
            P("section", "expert", None),
            P("section", None),
            P("section", None, "expert"),
            P("section", "expert", None),
            P("section", "expert", None),
            P("section", "expert", None),
            P("section", "expert", None),
        ),
        out_specs=P("section", "expert", None),
        check_vma=False,
    )
```

```python
import jax
import jax.numpy as jnp
from jax import lax
from jax.experimental import pallas as pl
from jax.experimental.pallas import tpu as pltpu
from jax.sharding import PartitionSpec as P

EXPERTS = 4
CAP = 68
EPSILON = 1e-06

TOK = 128
D = 2048
HALF = D // 2
BLOCK = 144
PAIR = 2 * BLOCK
SIDE = EXPERTS * BLOCK
STEP = 256
WIDE = 512
LANES = 4
QUARTER = 1024
PLANE = LANES * TOK
CHUNK = 32
PEERS = 16
SECTIONS = 8
OWN = 0
PART = TOK // 2
BF = jnp.bfloat16
F32 = jnp.float32
MESH = pl.DeviceIdType.MESH


def gelu_slope(x):
    scale = 0.7978845608028654
    square = x * x
    t = jnp.tanh(scale * x * (1.0 + 0.044715 * square))
    return 0.5 * (1.0 + t) + 0.5 * x * (1.0 - t * t) * (scale * (1.0 + 3 * 0.044715 * square))


def dot_nt(left, right):
    return lax.dot_general(left, right, (((1,), (1,)), ((), ())), preferred_element_type=F32)


def dot_nn(left, right):
    return jnp.dot(left, right, preferred_element_type=F32)


def at(start, size, unit=None):
    return pl.ds(pl.multiple_of(start, unit or size), size)


def rows_of(block):
    return pl.ds(block * BLOCK, BLOCK)


def tick_kernel(
    kvg, kvw, pend, enc, gain, ids, probs, w1, w2,
    out,
    W1, W2, GA, GB, QS, QR, QO, PF, RS, FIN, INC, INCX, NB, TK, WX, STX, LN, LS, XN, XS,
    GP, PH, SB, SR, PS, PR, CS, CR, NS, NR, NG,
    loc, ex_s, ex_r, pe_s, inc_r, kv_s, kv_r, zk_s, zk_r, q_s, q_r, rs_s, rs_r, fi_s, ix_s, ix_r,
    st_s, st_r, pa_s, pa_r, sb_s, sb_r, ss_s, ss_r, ps_s, ps_r, cr_s, cr_r, n_s, n_r,
):
    s = lax.axis_index("section")
    e = lax.axis_index("expert")
    xl, z, c = e // 8, (e // 2) % 4, e % 2
    oc, ox = 1 - c, 1 - xl
    zi = z + 1 - 2 * (z % 2)
    zc = 3 - z
    me = s * 2 + xl

    def dev(x, zz, cc, sec=s):
        return (sec, x * 8 + zz * 2 + cc)

    sib, partner, crossed = dev(xl, z, oc), dev(xl, zi, c), dev(xl, zc, c)
    lanes = [(xl, c), (xl, oc), (ox, c), (ox, oc)]
    group = [None, dev(ox, z, c), dev(xl, zc, c), dev(ox, zc, c)]
    my_cols, their_cols = at(c * HALF, HALF), at(oc * HALF, HALF)
    my_toks, their_toks = at(c * TOK, TOK), at(oc * TOK, TOK)

    def rc(src, dst, send, recv, where):
        return pltpu.make_async_remote_copy(
            src_ref=src, dst_ref=dst, send_sem=send, recv_sem=recv, device_id=where, device_id_type=MESH
        )

    sent, due = [], []

    def go(copy, key=None):
        copy.start()
        sent.append(copy)
        if key is not None:
            due.append((key, copy))

    def got(key, copy=None):
        for i, (k, own) in enumerate(due):
            if k == key:
                (copy or own).wait_recv()
                del due[i]
                return

    def gone(done):
        done.wait_send()
        sent[:] = [copy for copy in sent if copy is not done]

    load1 = pltpu.make_async_copy(w1, W1, loc.at[2, 0])
    load2 = pltpu.make_async_copy(w2, W2, loc.at[2, 1])

    barrier = pltpu.get_barrier_semaphore()

    def greet(where):
        pl.semaphore_signal(barrier, inc=1, device_id=where, device_id_type=MESH)

    for where in (sib, dev(ox, z, c), dev(ox, z, oc), partner, crossed, dev(ox, zc, c)):
        greet(where)

    def greet_peer(i, _):
        k = (me + i) % PEERS
        greet(dev(k % 2, z, c, k // 2))
        return 0

    lax.fori_loop(1, PEERS, greet_peer, 0)

    @pl.when(s < SECTIONS - 1)
    def _():
        greet(dev(xl, z, 0, s + 1))
        greet(dev(xl, z, 1, s + 1))

    @pl.when(s == SECTIONS - 1)
    def _():
        def greet_source(i, _):
            k = xl * 8 + i

            @pl.when(jnp.logical_not((k == me) & (c == 0)))
            def _():
                greet(dev(k % 2, z, 0, k // 2))

            greet(dev(k % 2, zi, 1, k // 2))
            return 0

        lax.fori_loop(0, PEERS // 2, greet_source, 0)

    zt = z + c * (zi - z)
    lane_t = me // 4
    xt, ct, sub = lane_t // 2, lane_t % 2, me % 4
    own_final = (s == SECTIONS - 1) & (xt == xl) & (zt == z)

    def lane_cols(x, cc):
        return at((x * 2 + cc) * QUARTER, QUARTER)

    def piece_rows(x, cc, half):
        return at((x * 2 + cc) * TOK + half * PART, PART)

    def kv_piece(i, r, half):
        source, held = ((kvg, GA), (kvw, GB))[i]
        x, cc = lanes[r]
        part = source.at[pl.ds(half * PART, PART), lane_cols(x, cc)]
        target = held.at[0, piece_rows(xl, c, half)]
        if r == 0:
            return pltpu.make_async_copy(part, target, loc.at[i, half])
        return rc(part, target, kv_s.at[i, r, half], kv_r.at[i, r, half], dev(x, z, cc))

    def z_piece(i, r, half):
        held, where = (GA, partner) if i == 0 else (GB, crossed)
        rows = piece_rows(*lanes[r], half)
        if r == 0:
            source = (kvg, kvw)[i].at[pl.ds(half * PART, PART), lane_cols(xl, c)]
        else:
            source = held.at[0, rows]
        return rc(source, held.at[1, rows], zk_s.at[i, r, half], zk_r.at[i, r, half], where)

    pl.semaphore_wait(
        barrier, 6 + PEERS - 1 + 2 * (s > 0).astype(jnp.int32) + 2 - own_final.astype(jnp.int32)
    )
    for i in range(2):
        for half in range(2):
            for r in (2, 3):
                go(kv_piece(i, r, half), ("kv", i, r, half))
    for i in range(2):
        for half in range(2):
            go(kv_piece(i, 1, half), ("kv", i, 1, half))
            go(z_piece(i, 0, half), ("zk", i, 0, half))
    for i in range(2):
        for half in range(2):
            kv_piece(i, 0, half).start()
    load1.start()
    load2.start()

    def norm_rows(j, _):
        rows = at(j * 32, 32)
        values = enc[rows, :].astype(F32)
        factor = lax.rsqrt(jnp.mean(values * values, axis=1, keepdims=True) + EPSILON)
        NB[rows, :] = (values * factor * gain[...]).astype(BF)
        return 0

    lax.fori_loop(0, TOK // 32, norm_rows, 0)
    zh = z // 2
    xd = (ids[...] // 2 != xl).astype(jnp.int32)
    zd = (ids[...] % 2 != zh).astype(jnp.int32)
    block = xd + 2 * zd
    which = lax.broadcasted_iota(jnp.int32, (16, TOK), 0)
    first, second = block[0:1, :] == which, block[1:2, :] == which
    used = (first | second).astype(F32)
    weight = jnp.where(first, probs[0:1, :], 0.0) + jnp.where(second, probs[1:2, :], 0.0)
    row, col = (lax.broadcasted_iota(jnp.int32, (TOK, TOK), i) for i in range(2))
    ahead = dot_nn(used.astype(BF), (row < col).astype(BF)) + (c * CAP).astype(F32)
    rest = jnp.zeros((TOK - 16, TOK), F32)
    ahead_t = jnp.concatenate([ahead, rest], axis=0).T
    used_t = jnp.concatenate([used, rest], axis=0).T
    slot = lax.broadcasted_iota(jnp.int32, (BLOCK, TOK), 0).astype(F32)
    column = lax.broadcasted_iota(jnp.int32, (TOK, STEP), 1).astype(F32)
    for p in range(EXPERTS):
        WX[c, rows_of(p), :] = jnp.where(slot == ahead[p:p + 1, :], weight[p:p + 1, :], 0.0)
        hit = jnp.where(column == ahead_t[:, p:p + 1], used_t[:, p:p + 1], 0.0)
        STX[c, :, pl.ds(p * STEP, STEP)] = hit.astype(BF)

    exchange = [
        rc(NB.at[:, their_cols], TK.at[my_toks], ex_s.at[0], ex_r.at[0], sib),
        rc(WX.at[c], WX.at[c], ex_s.at[1], ex_r.at[1], sib),
        rc(STX.at[c], STX.at[c], ex_s.at[2], ex_r.at[2], sib),
    ]
    for i in range(3):
        go(exchange[i], ("ex", i))
    TK[my_toks, :] = NB[:, my_cols]

    def kv_forward(i, r, half):
        got(("kv", i, r, half))
        go(z_piece(i, r, half), ("zk", i, r, half))

    for i in range(2):
        for half in range(2):
            kv_forward(i, 1, half)
    for r in (2, 3):
        kv_forward(0, r, 0)

    for i in range(3):
        got(("ex", i))

    def weights_of(p):
        both = jnp.concatenate([WX[0, rows_of(p), :], WX[1, rows_of(p), :]], axis=1)
        return both, (both > 0).astype(BF)

    for p in range(EXPERTS):
        _, hot = weights_of(p)
        slots = dot_nn(hot, TK[...]).astype(BF)
        if p == OWN:
            XN[0, c, rows_of(p)] = slots
        else:
            LN[p] = slots

    def stage1(a, p):
        source, held = ((LN, XN), (LS, XS))[a]
        return rc(source.at[p], held.at[0, c, rows_of(p)], st_s.at[a, p], st_r.at[a, p], group[p])

    def to_partner(a, p):
        held = (XN, XS)[a]
        return rc(held.at[0, c, rows_of(p)], held.at[1, c, rows_of(p)], pa_s.at[a, p], pa_r.at[a, p], partner)

    def to_sib(a, h, p):
        part = (XN, XS)[a].at[h, c, rows_of(p)]
        return rc(part, part, sb_s.at[a, h, p], sb_r.at[a, h, p], sib)

    def send_out(a, p):
        copy = stage1(a, p)
        go(copy, ("st", a, p))
        return copy

    def pass_on(a, p):
        go(to_partner(a, p), ("pa", a, p))
        go(to_sib(a, 0, p), ("sb", a, 0, p))

    def forward(a, p):
        got(("st", a, p))
        pass_on(a, p)

    def hand_over(a, p):
        got(("pa", a, p))
        go(to_sib(a, 1, p), ("sb", a, 1, p))

    def take(a, h, blocks):
        for p in blocks:
            part = (XN, XS)[a].at[h, oc, rows_of(p)]
            got(("sb", a, h, p), rc(part, part, sb_s.at[a, h, p], sb_r.at[a, h, p], sib))

    send_out(0, 1)
    send_out(0, 2)
    for r in (2, 3):
        kv_forward(0, r, 1)
    pass_on(0, OWN)
    for half in range(2):
        for r in (2, 3):
            kv_forward(1, r, half)
    send_out(0, 3)

    def pend_copy(core):
        return rc(pend.at[:, pl.ds(core * HALF, HALF)], INC.at[my_toks], pe_s.at[core], inc_r, dev(xl, z, core, s - 1))

    for i in range(2):
        for half in range(2):
            kv_piece(i, 0, half).wait()
            for r in range(LANES):
                if i == 0:
                    got(("zk", 0, r, half))

    def product(plane, p, store):
        for j in range(2):
            cols = pl.ds(j * STEP, STEP)
            store(p, cols, dot_nt(GA[plane], GB[p, cols, :]))

    def keep_theirs(p, cols, value):
        QS[p, :, cols] = value.astype(BF)

    def keep_mine(p, cols, value):
        PF[p, :, cols] = value

    def share(p, k):
        return rc(QO.at[p, at(k * CHUNK, CHUNK)], RS.at[p, me], rs_s.at[p, k], rs_r.at[p, me], dev(k % 2, z, c, k // 2))

    def share_in(p, k):
        return rc(RS.at[p, k], RS.at[p, k], rs_s.at[p, k], rs_r.at[p, k], dev(k % 2, z, c, k // 2))

    def spread(p):
        got(("swap", p))

        def add_core(j, _):
            rows = at(j * 64, 64)
            QO[p, rows, :] = (PF[p, rows, :] + QR[p, rows, :].astype(F32)).astype(BF)
            return 0

        lax.fori_loop(0, PLANE // 64, add_core, 0)

        def send_share(i, _):
            share(p, (me + i) % PEERS).start()
            return 0

        lax.fori_loop(1, PEERS, send_share, 0)
        RS[p, me] = QO[p, at(me * CHUNK, CHUNK), :]

    def half_product(p):
        product(oc, p, keep_theirs)
        go(rc(QS.at[p], QR.at[p], q_s.at[p], q_r.at[p], sib), ("swap", p))
        product(c, p, keep_mine)

    half_product(0)
    spread(0)
    for half in range(2):
        for r in range(LANES):
            got(("zk", 1, r, half))
    half_product(1)
    forward(0, 1)
    forward(0, 2)
    spread(1)

    @pl.when(s > 0)
    def _():
        pend_copy(0).start()
        pend_copy(1).start()

    def pre_act(h, first, rows):
        span = pl.ds(first, rows)

        def tile(j, _):
            cols = at(j * WIDE, WIDE)
            total = dot_nn(XN[h, 0, span], W1[pl.ds(0, HALF), cols]) + dot_nn(XN[h, 1, span], W1[pl.ds(HALF, HALF), cols])
            GP[h, span, cols] = gelu_slope(total).astype(BF)
            return 0

        lax.fori_loop(0, D // WIDE, tile, 0)

    load1.wait()
    take(0, 0, (0, 1))
    pre_act(0, 0, PAIR)
    forward(0, 3)

    def settle(p):
        def wait_share(i, _):
            share_in(p, (me + i) % PEERS).wait_recv()
            return 0

        lax.fori_loop(1, PEERS, wait_share, 0)
        total = RS[p, 0].astype(F32)
        for k in range(1, PEERS):
            total = total + RS[p, k].astype(F32)
        FIN[p] = total.astype(BF)
        for x in range(2):
            final(p, x, "start")

    def final(p, x, op):
        zz = z if p == 0 else zc
        source = FIN.at[p, :, pl.ds(x * STEP, STEP)]
        target = INC.at[at(ct * TOK + sub * CHUNK, CHUNK), at(zz * STEP, STEP)]
        away = rc(source, target, fi_s.at[p, x], inc_r, dev(xt, zt, x, SECTIONS - 1))
        at_home = jnp.logical_and(own_final, c == x)

        @pl.when(jnp.logical_not(at_home))
        def _():
            away.start() if op == "start" else away.wait_send()

        if op == "start":
            @pl.when(at_home)
            def _():
                pltpu.make_async_copy(source, target, inc_r).start()

    settle(0)
    hand_over(0, 0)
    hand_over(0, 1)
    settle(1)
    take(0, 0, (2, 3))
    pre_act(0, PAIR, PAIR)
    hand_over(0, 2)
    pltpu.make_async_copy(INC, INC, inc_r).wait()

    def scaled(p):
        both, hot = weights_of(p)
        return (dot_nn(hot, INC[...]) * jnp.sum(both, axis=1, keepdims=True)).astype(BF)

    XS[0, c, rows_of(OWN)] = scaled(OWN)
    pass_on(1, OWN)
    LS[1] = scaled(1)
    leaving = send_out(1, 1)
    LS[2] = scaled(2)
    send_out(1, 2)
    LS[3] = scaled(3)
    go(rc(INC.at[their_toks], INCX, ix_s, ix_r, sib), "inc")
    take(0, 1, (0, 1))
    pre_act(1, 0, PAIR)
    gone(leaving)
    send_out(1, 3)
    forward(1, 1)
    forward(1, 2)
    hand_over(0, 3)
    take(0, 1, (2, 3))
    pre_act(1, PAIR, PAIR)
    hand_over(1, 0)
    load2.wait()

    def hidden(h, first, rows):
        span = pl.ds(first, rows)

        def tile(j, _):
            cols = at(j * WIDE, WIDE)
            upstream = dot_nt(XS[h, 0, span], W2[cols, pl.ds(0, HALF)]) + dot_nt(XS[h, 1, span], W2[cols, pl.ds(HALF, HALF)])
            GP[h, span, cols] = (upstream * GP[h, span, cols].astype(F32)).astype(BF)
            return 0

        lax.fori_loop(0, D // WIDE, tile, 0)

    def pieces(h, first, rows):
        span = pl.ds(first, rows)
        for core, kept in ((oc, SB), (c, PH)):
            def tile(j, _, core=core, kept=kept):
                cols = at(j * WIDE, WIDE)
                kept[h, span, cols] = dot_nt(GP[h, span, :], W1[at(core * HALF + j * WIDE, WIDE), :]).astype(BF)
                return 0

            lax.fori_loop(0, HALF // WIDE, tile, 0)
            if kept is SB:
                i = 2 * h + first // PAIR
                go(rc(SB.at[h, span], SR.at[h, span], ss_s.at[i], ss_r.at[i], sib), ("ss", i))

    def partner_sum(p):
        return rc(PS.at[rows_of(p)], PR.at[rows_of(p)], ps_s.at[p], ps_r.at[p], partner)

    def add_cores(i, blocks):
        got(("ss", 2 + i))
        for p in blocks:
            def some(j, _, p=p):
                rows = at(p * BLOCK + j * 48, 48, 16)
                PS[rows, :] = (PH[1, rows, :].astype(F32) + SR[1, rows, :].astype(F32)).astype(BF)
                return 0

            lax.fori_loop(0, 3, some, 0)
            go(partner_sum(p), ("ps", p))

    take(1, 0, (0, 1))
    hidden(0, 0, PAIR)
    forward(1, 3)
    pieces(0, 0, PAIR)
    hand_over(1, 1)
    take(1, 1, (0, 1))
    hidden(1, 0, PAIR)
    hand_over(1, 2)
    pieces(1, 0, PAIR)
    add_cores(0, (1, 0))
    hand_over(1, 3)
    take(1, 1, (2, 3))
    hidden(1, PAIR, PAIR)
    pieces(1, PAIR, PAIR)
    add_cores(1, (3, 2))
    take(1, 0, (2, 3))
    hidden(0, PAIR, PAIR)

    def complete(p):
        got(("ps", p))
        held = CR if p == OWN else CS

        def some(j, _):
            rows = at(p * BLOCK + j * 48, 48, 16)
            value = PH[0, rows, :].astype(F32) + SR[0, rows, :].astype(F32) + PR[rows, :].astype(F32)
            held[p, at(j * 48, 48, 16), :] = value.astype(BF)
            return 0

        lax.fori_loop(0, 3, some, 0)
        if p != OWN:
            go(rc(CS.at[p], CR.at[p], cr_s.at[p], cr_r.at[p], group[p]), ("cr", p))

    def gathered(core, p):
        return dot_nn(STX[core, :, pl.ds(p * STEP, BLOCK)], CR[p])

    got(("ss", 0))
    complete(1)
    pieces(0, PAIR, PAIR)
    complete(OWN)
    got(("ss", 1))
    complete(3)
    got(("cr", 1))
    NS[...] = gathered(oc, OWN) + gathered(oc, 1)
    NG[...] = gathered(c, OWN) + gathered(c, 1)
    complete(2)
    got(("cr", 3))
    NS[...] = NS[...] + gathered(oc, 3)
    NG[...] = NG[...] + gathered(c, 3)
    got(("cr", 2))
    NS[...] = NS[...] + gathered(oc, 2)
    go(rc(NS, NR, n_s, n_r, sib), "last")
    NG[...] = NG[...] + gathered(c, 2)
    got("inc")
    got("last")

    def finish(j, _):
        rows = at(j * 32, 32)
        mine_x, their_x = enc[rows, my_cols].astype(F32), enc[rows, their_cols].astype(F32)
        mine_g, their_g = NG[rows, :] * gain[:, my_cols], NR[rows, :] * gain[:, their_cols]
        power = jnp.sum(mine_x * mine_x, axis=1, keepdims=True) + jnp.sum(their_x * their_x, axis=1, keepdims=True)
        factor = lax.rsqrt(power * (1.0 / D) + EPSILON)
        along = jnp.sum(mine_g * mine_x, axis=1, keepdims=True) + jnp.sum(their_g * their_x, axis=1, keepdims=True)
        pull = along * factor * factor * factor * (1.0 / D)
        incoming = INC[at(c * TOK + j * 32, 32), :].astype(F32)
        out[rows, my_cols] = (incoming + mine_g * factor - mine_x * pull).astype(BF)
        out[rows, their_cols] = (INCX[rows, :].astype(F32) + their_g * factor - their_x * pull).astype(BF)
        return 0

    lax.fori_loop(0, TOK // 32, finish, 0)

    @pl.when(s > 0)
    def _():
        pend_copy(0).wait_send()
        pend_copy(1).wait_send()

    def sent_share(i, _):
        for p in range(2):
            share(p, (me + i) % PEERS).wait_send()
        return 0

    lax.fori_loop(1, PEERS, sent_share, 0)
    for p in range(2):
        for x in range(2):
            final(p, x, "wait")
    for copy in sent:
        copy.wait_send()


def tick(kvg, kvw, pend, enc, gain, ids, probs, w1, w2):
    any_place = pl.BlockSpec(memory_space=pl.ANY)
    vmem = pl.BlockSpec(memory_space=pltpu.VMEM)
    dma = pltpu.SemaphoreType.DMA
    V = pltpu.VMEM
    scratch = [
        V((D, D), BF), V((D, D), BF),
        V((2, PLANE, QUARTER), BF), V((2, PLANE, QUARTER), BF),
        V((2, PLANE, PLANE), BF), V((2, PLANE, PLANE), BF), V((2, PLANE, PLANE), BF), V((2, PLANE, PLANE), F32),
        V((2, PEERS, CHUNK, PLANE), BF), V((2, CHUNK, PLANE), BF),
        V((2 * TOK, HALF), BF), V((TOK, HALF), BF), V((TOK, D), BF), V((2 * TOK, HALF), BF),
        V((2, SIDE, TOK), F32), V((2, TOK, EXPERTS * STEP), BF),
        V((EXPERTS, BLOCK, HALF), BF), V((EXPERTS, BLOCK, HALF), BF),
        V((2, 2, SIDE, HALF), BF), V((2, 2, SIDE, HALF), BF),
        V((2, SIDE, D), BF),
        V((2, SIDE, HALF), BF), V((2, SIDE, HALF), BF), V((2, SIDE, HALF), BF),
        V((SIDE, HALF), BF), V((SIDE, HALF), BF),
        V((EXPERTS, BLOCK, HALF), BF), V((EXPERTS, BLOCK, HALF), BF),
        V((TOK, HALF), F32), V((TOK, HALF), F32), V((TOK, HALF), F32),
        dma((3, 2)), dma((3,)), dma((3,)), dma((2,)), dma, dma((2, 4, 2)), dma((2, 4, 2)), dma((2, 4, 2)), dma((2, 4, 2)),
        dma((2,)), dma((2,)), dma((2, PEERS)), dma((2, PEERS)), dma((2, 2)), dma, dma,
        dma((2, 4)), dma((2, 4)), dma((2, 4)), dma((2, 4)), dma((2, 2, 4)), dma((2, 2, 4)),
        dma((4,)), dma((4,)), dma((4,)), dma((4,)), dma((4,)), dma((4,)), dma, dma,
    ]
    return pl.pallas_call(
        tick_kernel,
        out_shape=jax.ShapeDtypeStruct((TOK, D), BF),
        in_specs=[any_place] * 3 + [vmem] * 4 + [any_place] * 2,
        out_specs=vmem,
        scratch_shapes=scratch,
        compiler_params=pltpu.CompilerParams(
            collective_id=0, has_side_effects=True, vmem_limit_bytes=62 * 1024 * 1024
        ),
        name="tick",
    )(kvg, kvw, pend, enc, gain, ids, probs, w1, w2)


def body(
    kv_grads, kv_weight, enc_inputs, enc_gain, enc_w1, enc_w2, route_ids, route_probs, pending_grads
):
    return tick(
        kv_grads[0], kv_weight[0], pending_grads[0], enc_inputs[0], enc_gain, route_ids[0].T, route_probs[0].T,
        enc_w1[0], enc_w2[0],
    )[None]


def solution(mesh):
    return jax.shard_map(
        body,
        mesh=mesh,
        in_specs=(
            P("section", "expert", None),
            P("section", "expert", None),
            P("section", "expert", None),
            P("section", None),
            P("section", None, "expert"),
            P("section", "expert", None),
            P("section", "expert", None),
            P("section", "expert", None),
            P("section", "expert", None),
        ),
        out_specs=P("section", "expert", None),
        check_vma=False,
    )
```

```python
import jax
import jax.numpy as jnp
from jax import lax
from jax.experimental import pallas as pl
from jax.experimental.pallas import tpu as pltpu
from jax.sharding import PartitionSpec as P

EXPERTS = 4
CAP = 68
EPSILON = 1e-06

TOK = 128
D = 2048
HALF = D // 2
BLOCK = 144
PAIR = 2 * BLOCK
SIDE = EXPERTS * BLOCK
STEP = 256
WIDE = 512
LANES = 4
QUARTER = 1024
PLANE = LANES * TOK
CHUNK = 32
PEERS = 16
SECTIONS = 8
OWN = 0
PART = TOK // 2
BF = jnp.bfloat16
F32 = jnp.float32
MESH = pl.DeviceIdType.MESH


def gelu_slope(x):
    scale = 0.7978845608028654
    square = x * x
    t = jnp.tanh(scale * x * (1.0 + 0.044715 * square))
    return 0.5 * (1.0 + t) + 0.5 * x * (1.0 - t * t) * (scale * (1.0 + 3 * 0.044715 * square))


def dot_nt(left, right):
    return lax.dot_general(left, right, (((1,), (1,)), ((), ())), preferred_element_type=F32)


def dot_nn(left, right):
    return jnp.dot(left, right, preferred_element_type=F32)


def at(start, size, unit=None):
    return pl.ds(pl.multiple_of(start, unit or size), size)


def rows_of(block):
    return pl.ds(block * BLOCK, BLOCK)


def tick_kernel(
    kvg, kvw, pend, enc, gain, ids, probs, w1, w2,
    out,
    W1, W2, GA, GB, QS, QR, QO, PF, RS, FIN, INC, INCX, NB, TK, WX, STX, LN, LS, XN, XS,
    GP, PH, SB, SR, PS, PR, CS, CR, NS, NR, NG,
    loc, ex_s, ex_r, pe_s, inc_r, kv_s, kv_r, zk_s, zk_r, q_s, q_r, rs_s, rs_r, fi_s, ix_s, ix_r,
    st_s, st_r, pa_s, pa_r, sb_s, sb_r, ss_s, ss_r, ps_s, ps_r, cr_s, cr_r, n_s, n_r,
):
    s = lax.axis_index("section")
    e = lax.axis_index("expert")
    xl, z, c = e // 8, (e // 2) % 4, e % 2
    oc, ox = 1 - c, 1 - xl
    zi = z + 1 - 2 * (z % 2)
    zc = 3 - z
    me = s * 2 + xl

    def dev(x, zz, cc, sec=s):
        return (sec, x * 8 + zz * 2 + cc)

    sib, partner, crossed = dev(xl, z, oc), dev(xl, zi, c), dev(xl, zc, c)
    lanes = [(xl, c), (xl, oc), (ox, c), (ox, oc)]
    group = [None, dev(ox, z, c), dev(xl, zc, c), dev(ox, zc, c)]
    my_cols, their_cols = at(c * HALF, HALF), at(oc * HALF, HALF)
    my_toks, their_toks = at(c * TOK, TOK), at(oc * TOK, TOK)

    def rc(src, dst, send, recv, where):
        return pltpu.make_async_remote_copy(
            src_ref=src, dst_ref=dst, send_sem=send, recv_sem=recv, device_id=where, device_id_type=MESH
        )

    sent, due = [], []

    def go(copy, key=None):
        copy.start()
        sent.append(copy)
        if key is not None:
            due.append((key, copy))

    def got(key, copy=None):
        for i, (k, own) in enumerate(due):
            if k == key:
                (copy or own).wait_recv()
                del due[i]
                return

    def gone(done):
        done.wait_send()
        sent[:] = [copy for copy in sent if copy is not done]

    load1 = pltpu.make_async_copy(w1, W1, loc.at[2, 0])
    load2 = pltpu.make_async_copy(w2, W2, loc.at[2, 1])

    barrier = pltpu.get_barrier_semaphore()

    def greet(where):
        pl.semaphore_signal(barrier, inc=1, device_id=where, device_id_type=MESH)

    for where in (sib, dev(ox, z, c), dev(ox, z, oc), partner, crossed, dev(ox, zc, c)):
        greet(where)

    def greet_peer(i, _):
        k = (me + i) % PEERS
        greet(dev(k % 2, z, c, k // 2))
        return 0

    lax.fori_loop(1, PEERS, greet_peer, 0)

    @pl.when(s < SECTIONS - 1)
    def _():
        greet(dev(xl, z, 0, s + 1))
        greet(dev(xl, z, 1, s + 1))

    @pl.when(s == SECTIONS - 1)
    def _():
        def greet_source(i, _):
            k = i * 2 + xl

            @pl.when(jnp.logical_not((k == me) & (c == 0)))
            def _():
                greet(dev(k % 2, z, 0, k // 2))

            greet(dev(k % 2, zi, 1, k // 2))
            return 0

        lax.fori_loop(0, PEERS // 2, greet_source, 0)

    zt = z + c * (zi - z)
    xt, ct, sub = xl, s // 4, s % 4
    own_final = (s == SECTIONS - 1) & (xt == xl) & (zt == z)

    def lane_cols(x, cc):
        return at((x * 2 + cc) * QUARTER, QUARTER)

    def piece_rows(x, cc, half):
        return at((x * 2 + cc) * TOK + half * PART, PART)

    def kv_piece(i, r, half):
        source, held = ((kvg, GA), (kvw, GB))[i]
        x, cc = lanes[r]
        part = source.at[pl.ds(half * PART, PART), lane_cols(x, cc)]
        target = held.at[0, piece_rows(xl, c, half)]
        if r == 0:
            return pltpu.make_async_copy(part, target, loc.at[i, half])
        return rc(part, target, kv_s.at[i, r, half], kv_r.at[i, r, half], dev(x, z, cc))

    def z_piece(i, r, half):
        held, where = (GA, partner) if i == 0 else (GB, crossed)
        rows = piece_rows(*lanes[r], half)
        if r == 0:
            source = (kvg, kvw)[i].at[pl.ds(half * PART, PART), lane_cols(xl, c)]
        else:
            source = held.at[0, rows]
        return rc(source, held.at[1, rows], zk_s.at[i, r, half], zk_r.at[i, r, half], where)

    pl.semaphore_wait(
        barrier, 6 + PEERS - 1 + 2 * (s > 0).astype(jnp.int32) + 2 - own_final.astype(jnp.int32)
    )
    for i in range(2):
        for half in range(2):
            for r in (2, 3):
                go(kv_piece(i, r, half), ("kv", i, r, half))
    for i in range(2):
        for half in range(2):
            go(kv_piece(i, 1, half), ("kv", i, 1, half))
            go(z_piece(i, 0, half), ("zk", i, 0, half))
    for i in range(2):
        for half in range(2):
            kv_piece(i, 0, half).start()
    load1.start()
    load2.start()

    def norm_rows(j, _):
        rows = at(j * 32, 32)
        values = enc[rows, :].astype(F32)
        factor = lax.rsqrt(jnp.mean(values * values, axis=1, keepdims=True) + EPSILON)
        NB[rows, :] = (values * factor * gain[...]).astype(BF)
        return 0

    lax.fori_loop(0, TOK // 32, norm_rows, 0)
    zh = z // 2
    xd = (ids[...] // 2 != xl).astype(jnp.int32)
    zd = (ids[...] % 2 != zh).astype(jnp.int32)
    block = xd + 2 * zd
    which = lax.broadcasted_iota(jnp.int32, (16, TOK), 0)
    first, second = block[0:1, :] == which, block[1:2, :] == which
    used = (first | second).astype(F32)
    weight = jnp.where(first, probs[0:1, :], 0.0) + jnp.where(second, probs[1:2, :], 0.0)
    row, col = (lax.broadcasted_iota(jnp.int32, (TOK, TOK), i) for i in range(2))
    ahead = dot_nn(used.astype(BF), (row < col).astype(BF)) + (c * CAP).astype(F32)
    rest = jnp.zeros((TOK - 16, TOK), F32)
    ahead_t = jnp.concatenate([ahead, rest], axis=0).T
    used_t = jnp.concatenate([used, rest], axis=0).T
    slot = lax.broadcasted_iota(jnp.int32, (BLOCK, TOK), 0).astype(F32)
    column = lax.broadcasted_iota(jnp.int32, (TOK, STEP), 1).astype(F32)
    for p in range(EXPERTS):
        WX[c, rows_of(p), :] = jnp.where(slot == ahead[p:p + 1, :], weight[p:p + 1, :], 0.0)
        hit = jnp.where(column == ahead_t[:, p:p + 1], used_t[:, p:p + 1], 0.0)
        STX[c, :, pl.ds(p * STEP, STEP)] = hit.astype(BF)

    exchange = [
        rc(NB.at[:, their_cols], TK.at[my_toks], ex_s.at[0], ex_r.at[0], sib),
        rc(WX.at[c], WX.at[c], ex_s.at[1], ex_r.at[1], sib),
        rc(STX.at[c], STX.at[c], ex_s.at[2], ex_r.at[2], sib),
    ]
    for i in range(3):
        go(exchange[i], ("ex", i))
    TK[my_toks, :] = NB[:, my_cols]

    def kv_forward(i, r, half):
        got(("kv", i, r, half))
        go(z_piece(i, r, half), ("zk", i, r, half))

    for i in range(2):
        for half in range(2):
            kv_forward(i, 1, half)
    for r in (2, 3):
        kv_forward(0, r, 0)

    for i in range(3):
        got(("ex", i))

    def weights_of(p):
        both = jnp.concatenate([WX[0, rows_of(p), :], WX[1, rows_of(p), :]], axis=1)
        return both, (both > 0).astype(BF)

    for p in range(EXPERTS):
        _, hot = weights_of(p)
        slots = dot_nn(hot, TK[...]).astype(BF)
        if p == OWN:
            XN[0, c, rows_of(p)] = slots
        else:
            LN[p] = slots

    def stage1(a, p):
        source, held = ((LN, XN), (LS, XS))[a]
        return rc(source.at[p], held.at[0, c, rows_of(p)], st_s.at[a, p], st_r.at[a, p], group[p])

    def to_partner(a, p):
        held = (XN, XS)[a]
        return rc(held.at[0, c, rows_of(p)], held.at[1, c, rows_of(p)], pa_s.at[a, p], pa_r.at[a, p], partner)

    def to_sib(a, h, p):
        part = (XN, XS)[a].at[h, c, rows_of(p)]
        return rc(part, part, sb_s.at[a, h, p], sb_r.at[a, h, p], sib)

    def send_out(a, p):
        copy = stage1(a, p)
        go(copy, ("st", a, p))
        return copy

    def pass_on(a, p):
        go(to_partner(a, p), ("pa", a, p))
        go(to_sib(a, 0, p), ("sb", a, 0, p))

    def forward(a, p):
        got(("st", a, p))
        pass_on(a, p)

    def hand_over(a, p):
        got(("pa", a, p))
        go(to_sib(a, 1, p), ("sb", a, 1, p))

    def take(a, h, blocks):
        for p in blocks:
            part = (XN, XS)[a].at[h, oc, rows_of(p)]
            got(("sb", a, h, p), rc(part, part, sb_s.at[a, h, p], sb_r.at[a, h, p], sib))

    send_out(0, 1)
    send_out(0, 2)
    for r in (2, 3):
        kv_forward(0, r, 1)
    pass_on(0, OWN)
    for r in (2, 3):
        kv_forward(1, r, 0)
    forward(0, 2)
    for r in (2, 3):
        kv_forward(1, r, 1)

    def pend_copy(core):
        return rc(pend.at[:, pl.ds(core * HALF, HALF)], INC.at[my_toks], pe_s.at[core], inc_r, dev(xl, z, core, s - 1))

    for i in range(2):
        for half in range(2):
            kv_piece(i, 0, half).wait()
            for r in range(LANES):
                if i == 0:
                    got(("zk", 0, r, half))

    def product(plane, p, store):
        for j in range(2):
            cols = pl.ds(j * STEP, STEP)
            store(p, cols, dot_nt(GA[plane], GB[p, cols, :]))

    def keep_theirs(p, cols, value):
        QS[p, :, cols] = value.astype(BF)

    def keep_mine(p, cols, value):
        PF[p, :, cols] = value

    def chunk_of(k):
        return at((k % 2 * 8 + k // 2) * CHUNK, CHUNK)

    def share(p, k):
        return rc(QO.at[p, chunk_of(k)], RS.at[p, me], rs_s.at[p, k], rs_r.at[p, me], dev(k % 2, z, c, k // 2))

    def share_in(p, k):
        return rc(RS.at[p, k], RS.at[p, k], rs_s.at[p, k], rs_r.at[p, k], dev(k % 2, z, c, k // 2))

    def spread(p):
        got(("swap", p))

        def add_core(j, _):
            rows = at(j * 64, 64)
            QO[p, rows, :] = (PF[p, rows, :] + QR[p, rows, :].astype(F32)).astype(BF)
            return 0

        lax.fori_loop(0, PLANE // 64, add_core, 0)

        def send_share(i, _):
            share(p, (me + i) % PEERS).start()
            return 0

        lax.fori_loop(1, PEERS, send_share, 0)
        RS[p, me] = QO[p, chunk_of(me), :]

    def half_product(p):
        product(oc, p, keep_theirs)
        go(rc(QS.at[p], QR.at[p], q_s.at[p], q_r.at[p], sib), ("swap", p))
        product(c, p, keep_mine)

    half_product(0)
    spread(0)
    forward(0, 1)
    send_out(0, 3)
    for half in range(2):
        for r in range(LANES):
            got(("zk", 1, r, half))
    half_product(1)
    spread(1)

    @pl.when(s > 0)
    def _():
        pend_copy(0).start()
        pend_copy(1).start()

    def pre_act(h, first, rows):
        span = pl.ds(first, rows)

        def tile(j, _):
            cols = at(j * WIDE, WIDE)
            total = dot_nn(XN[h, 0, span], W1[pl.ds(0, HALF), cols]) + dot_nn(XN[h, 1, span], W1[pl.ds(HALF, HALF), cols])
            GP[h, span, cols] = gelu_slope(total).astype(BF)
            return 0

        lax.fori_loop(0, D // WIDE, tile, 0)

    load1.wait()

    def settle(p):
        def wait_share(i, _):
            share_in(p, (me + i) % PEERS).wait_recv()
            return 0

        lax.fori_loop(1, PEERS, wait_share, 0)
        total = RS[p, 0].astype(F32)
        for k in range(1, PEERS):
            total = total + RS[p, k].astype(F32)
        FIN[p] = total.astype(BF)
        for x in range(2):
            final(p, x, "start")

    def final(p, x, op):
        zz = z if p == 0 else zc
        source = FIN.at[p, :, pl.ds(x * STEP, STEP)]
        target = INC.at[at(ct * TOK + sub * CHUNK, CHUNK), at(zz * STEP, STEP)]
        away = rc(source, target, fi_s.at[p, x], inc_r, dev(xt, zt, x, SECTIONS - 1))
        at_home = jnp.logical_and(own_final, c == x)

        @pl.when(jnp.logical_not(at_home))
        def _():
            away.start() if op == "start" else away.wait_send()

        if op == "start":
            @pl.when(at_home)
            def _():
                pltpu.make_async_copy(source, target, inc_r).start()

    settle(0)
    forward(0, 3)
    take(0, 0, (0, 1))
    pre_act(0, 0, PAIR)
    hand_over(0, 0)
    hand_over(0, 2)
    take(0, 0, (2, 3))
    pre_act(0, PAIR, PAIR)
    settle(1)
    hand_over(0, 1)
    take(0, 1, (0, 1))
    pre_act(1, 0, PAIR)
    hand_over(0, 3)
    take(0, 1, (2, 3))
    pre_act(1, PAIR, PAIR)
    pltpu.make_async_copy(INC, INC, inc_r).wait()

    def scaled(p):
        both, hot = weights_of(p)
        return (dot_nn(hot, INC[...]) * jnp.sum(both, axis=1, keepdims=True)).astype(BF)

    XS[0, c, rows_of(OWN)] = scaled(OWN)
    pass_on(1, OWN)
    LS[1] = scaled(1)
    leaving = send_out(1, 1)
    LS[2] = scaled(2)
    send_out(1, 2)
    LS[3] = scaled(3)
    go(rc(INC.at[their_toks], INCX, ix_s, ix_r, sib), "inc")
    gone(leaving)
    send_out(1, 3)
    forward(1, 1)
    forward(1, 2)
    hand_over(1, 0)
    load2.wait()

    def hidden(h, first, rows):
        span = pl.ds(first, rows)

        def tile(j, _):
            cols = at(j * WIDE, WIDE)
            upstream = dot_nt(XS[h, 0, span], W2[cols, pl.ds(0, HALF)]) + dot_nt(XS[h, 1, span], W2[cols, pl.ds(HALF, HALF)])
            GP[h, span, cols] = (upstream * GP[h, span, cols].astype(F32)).astype(BF)
            return 0

        lax.fori_loop(0, D // WIDE, tile, 0)

    def pieces(h, first, rows):
        span = pl.ds(first, rows)
        for core, kept in ((oc, SB), (c, PH)):
            def tile(j, _, core=core, kept=kept):
                cols = at(j * WIDE, WIDE)
                kept[h, span, cols] = dot_nt(GP[h, span, :], W1[at(core * HALF + j * WIDE, WIDE), :]).astype(BF)
                return 0

            lax.fori_loop(0, HALF // WIDE, tile, 0)
            if kept is SB:
                i = 2 * h + first // PAIR
                go(rc(SB.at[h, span], SR.at[h, span], ss_s.at[i], ss_r.at[i], sib), ("ss", i))

    def partner_sum(p):
        return rc(PS.at[rows_of(p)], PR.at[rows_of(p)], ps_s.at[p], ps_r.at[p], partner)

    def add_cores(i, blocks):
        got(("ss", 2 + i))
        for p in blocks:
            def some(j, _, p=p):
                rows = at(p * BLOCK + j * 48, 48, 16)
                PS[rows, :] = (PH[1, rows, :].astype(F32) + SR[1, rows, :].astype(F32)).astype(BF)
                return 0

            lax.fori_loop(0, 3, some, 0)
            go(partner_sum(p), ("ps", p))

    take(1, 0, (0, 1))
    hidden(0, 0, PAIR)
    forward(1, 3)
    pieces(0, 0, PAIR)
    hand_over(1, 1)
    take(1, 1, (0, 1))
    hidden(1, 0, PAIR)
    hand_over(1, 2)
    pieces(1, 0, PAIR)
    add_cores(0, (1, 0))
    take(1, 0, (2, 3))
    hidden(0, PAIR, PAIR)
    hand_over(1, 3)
    pieces(0, PAIR, PAIR)
    take(1, 1, (2, 3))
    hidden(1, PAIR, PAIR)

    def complete(p):
        got(("ps", p))
        held = CR if p == OWN else CS

        def some(j, _):
            rows = at(p * BLOCK + j * 48, 48, 16)
            value = PH[0, rows, :].astype(F32) + SR[0, rows, :].astype(F32) + PR[rows, :].astype(F32)
            held[p, at(j * 48, 48, 16), :] = value.astype(BF)
            return 0

        lax.fori_loop(0, 3, some, 0)
        if p != OWN:
            go(rc(CS.at[p], CR.at[p], cr_s.at[p], cr_r.at[p], group[p]), ("cr", p))

    def gathered(core, p):
        return dot_nn(STX[core, :, pl.ds(p * STEP, BLOCK)], CR[p])

    got(("ss", 0))
    complete(1)
    pieces(1, PAIR, PAIR)
    add_cores(1, (3, 2))
    complete(OWN)
    got(("ss", 1))
    complete(3)
    got(("cr", 1))
    NS[...] = gathered(oc, OWN) + gathered(oc, 1)
    NG[...] = gathered(c, OWN) + gathered(c, 1)
    complete(2)
    got(("cr", 3))
    NS[...] = NS[...] + gathered(oc, 3)
    NG[...] = NG[...] + gathered(c, 3)
    got(("cr", 2))
    NS[...] = NS[...] + gathered(oc, 2)
    go(rc(NS, NR, n_s, n_r, sib), "last")
    NG[...] = NG[...] + gathered(c, 2)
    got("inc")
    got("last")

    def finish(j, _):
        rows = at(j * 32, 32)
        mine_x, their_x = enc[rows, my_cols].astype(F32), enc[rows, their_cols].astype(F32)
        mine_g, their_g = NG[rows, :] * gain[:, my_cols], NR[rows, :] * gain[:, their_cols]
        power = jnp.sum(mine_x * mine_x, axis=1, keepdims=True) + jnp.sum(their_x * their_x, axis=1, keepdims=True)
        factor = lax.rsqrt(power * (1.0 / D) + EPSILON)
        along = jnp.sum(mine_g * mine_x, axis=1, keepdims=True) + jnp.sum(their_g * their_x, axis=1, keepdims=True)
        pull = along * factor * factor * factor * (1.0 / D)
        incoming = INC[at(c * TOK + j * 32, 32), :].astype(F32)
        out[rows, my_cols] = (incoming + mine_g * factor - mine_x * pull).astype(BF)
        out[rows, their_cols] = (INCX[rows, :].astype(F32) + their_g * factor - their_x * pull).astype(BF)
        return 0

    lax.fori_loop(0, TOK // 32, finish, 0)

    @pl.when(s > 0)
    def _():
        pend_copy(0).wait_send()
        pend_copy(1).wait_send()

    def sent_share(i, _):
        for p in range(2):
            share(p, (me + i) % PEERS).wait_send()
        return 0

    lax.fori_loop(1, PEERS, sent_share, 0)
    for p in range(2):
        for x in range(2):
            final(p, x, "wait")
    for copy in sent:
        copy.wait_send()


def tick(kvg, kvw, pend, enc, gain, ids, probs, w1, w2):
    any_place = pl.BlockSpec(memory_space=pl.ANY)
    vmem = pl.BlockSpec(memory_space=pltpu.VMEM)
    dma = pltpu.SemaphoreType.DMA
    V = pltpu.VMEM
    scratch = [
        V((D, D), BF), V((D, D), BF),
        V((2, PLANE, QUARTER), BF), V((2, PLANE, QUARTER), BF),
        V((2, PLANE, PLANE), BF), V((2, PLANE, PLANE), BF), V((2, PLANE, PLANE), BF), V((2, PLANE, PLANE), F32),
        V((2, PEERS, CHUNK, PLANE), BF), V((2, CHUNK, PLANE), BF),
        V((2 * TOK, HALF), BF), V((TOK, HALF), BF), V((TOK, D), BF), V((2 * TOK, HALF), BF),
        V((2, SIDE, TOK), F32), V((2, TOK, EXPERTS * STEP), BF),
        V((EXPERTS, BLOCK, HALF), BF), V((EXPERTS, BLOCK, HALF), BF),
        V((2, 2, SIDE, HALF), BF), V((2, 2, SIDE, HALF), BF),
        V((2, SIDE, D), BF),
        V((2, SIDE, HALF), BF), V((2, SIDE, HALF), BF), V((2, SIDE, HALF), BF),
        V((SIDE, HALF), BF), V((SIDE, HALF), BF),
        V((EXPERTS, BLOCK, HALF), BF), V((EXPERTS, BLOCK, HALF), BF),
        V((TOK, HALF), F32), V((TOK, HALF), F32), V((TOK, HALF), F32),
        dma((3, 2)), dma((3,)), dma((3,)), dma((2,)), dma, dma((2, 4, 2)), dma((2, 4, 2)), dma((2, 4, 2)), dma((2, 4, 2)),
        dma((2,)), dma((2,)), dma((2, PEERS)), dma((2, PEERS)), dma((2, 2)), dma, dma,
        dma((2, 4)), dma((2, 4)), dma((2, 4)), dma((2, 4)), dma((2, 2, 4)), dma((2, 2, 4)),
        dma((4,)), dma((4,)), dma((4,)), dma((4,)), dma((4,)), dma((4,)), dma, dma,
    ]
    return pl.pallas_call(
        tick_kernel,
        out_shape=jax.ShapeDtypeStruct((TOK, D), BF),
        in_specs=[any_place] * 3 + [vmem] * 4 + [any_place] * 2,
        out_specs=vmem,
        scratch_shapes=scratch,
        compiler_params=pltpu.CompilerParams(
            collective_id=0, has_side_effects=True, vmem_limit_bytes=62 * 1024 * 1024
        ),
        name="tick",
    )(kvg, kvw, pend, enc, gain, ids, probs, w1, w2)


def body(
    kv_grads, kv_weight, enc_inputs, enc_gain, enc_w1, enc_w2, route_ids, route_probs, pending_grads
):
    return tick(
        kv_grads[0], kv_weight[0], pending_grads[0], enc_inputs[0], enc_gain, route_ids[0].T, route_probs[0].T,
        enc_w1[0], enc_w2[0],
    )[None]


def solution(mesh):
    return jax.shard_map(
        body,
        mesh=mesh,
        in_specs=(
            P("section", "expert", None),
            P("section", "expert", None),
            P("section", "expert", None),
            P("section", None),
            P("section", None, "expert"),
            P("section", "expert", None),
            P("section", "expert", None),
            P("section", "expert", None),
            P("section", "expert", None),
        ),
        out_specs=P("section", "expert", None),
        check_vma=False,
    )
```

```python
import jax
import jax.numpy as jnp
from jax import lax
from jax.experimental import pallas as pl
from jax.experimental.pallas import tpu as pltpu
from jax.sharding import PartitionSpec as P

EXPERTS = 4
CAP = 68
EPSILON = 1e-06

TOK = 128
D = 2048
HALF = D // 2
BLOCK = 144
PAIR = 2 * BLOCK
SIDE = EXPERTS * BLOCK
STEP = 256
WIDE = 512
LANES = 4
QUARTER = 1024
PLANE = LANES * TOK
CHUNK = 32
PEERS = 16
SECTIONS = 8
OWN = 0
PART = TOK // 2
BF = jnp.bfloat16
F32 = jnp.float32
MESH = pl.DeviceIdType.MESH


def gelu_slope(x):
    scale = 0.7978845608028654
    square = x * x
    t = jnp.tanh(scale * x * (1.0 + 0.044715 * square))
    return 0.5 * (1.0 + t) + 0.5 * x * (1.0 - t * t) * (scale * (1.0 + 3 * 0.044715 * square))


def dot_nt(left, right):
    return lax.dot_general(left, right, (((1,), (1,)), ((), ())), preferred_element_type=F32)


def dot_nn(left, right):
    return jnp.dot(left, right, preferred_element_type=F32)


def at(start, size, unit=None):
    return pl.ds(pl.multiple_of(start, unit or size), size)


def rows_of(block):
    return pl.ds(block * BLOCK, BLOCK)


def tick_kernel(
    kvg, kvw, pend, enc, gain, ids, probs, w1, w2,
    out,
    W1, W2, GA, GB, QS, QR, QO, PF, RS, FIN, INC, INCX, NB, TK, WX, STX, LN, LS, XN, XS,
    GP, PH, SB, SR, PS, PR, CS, CR, NS, NR, NG,
    loc, ex_s, ex_r, pe_s, inc_r, kv_s, kv_r, zk_s, zk_r, q_s, q_r, rs_s, rs_r, fi_s, ix_s, ix_r,
    st_s, st_r, pa_s, pa_r, sb_s, sb_r, ss_s, ss_r, ps_s, ps_r, cr_s, cr_r, n_s, n_r,
):
    s = lax.axis_index("section")
    e = lax.axis_index("expert")
    xl, z, c = e // 8, (e // 2) % 4, e % 2
    oc, ox = 1 - c, 1 - xl
    zi = z + 1 - 2 * (z % 2)
    zc = 3 - z
    me = s * 2 + xl

    def dev(x, zz, cc, sec=s):
        return (sec, x * 8 + zz * 2 + cc)

    sib, partner, crossed = dev(xl, z, oc), dev(xl, zi, c), dev(xl, zc, c)
    lanes = [(xl, c), (xl, oc), (ox, c), (ox, oc)]
    group = [None, dev(ox, z, c), dev(xl, zc, c), dev(ox, zc, c)]
    my_cols, their_cols = at(c * HALF, HALF), at(oc * HALF, HALF)
    my_toks, their_toks = at(c * TOK, TOK), at(oc * TOK, TOK)

    def rc(src, dst, send, recv, where):
        return pltpu.make_async_remote_copy(
            src_ref=src, dst_ref=dst, send_sem=send, recv_sem=recv, device_id=where, device_id_type=MESH
        )

    sent, due = [], []

    def go(copy, key=None):
        copy.start()
        sent.append(copy)
        if key is not None:
            due.append((key, copy))

    def got(key, copy=None):
        for i, (k, own) in enumerate(due):
            if k == key:
                (copy or own).wait_recv()
                del due[i]
                return

    def gone(done):
        done.wait_send()
        sent[:] = [copy for copy in sent if copy is not done]

    load1 = pltpu.make_async_copy(w1, W1, loc.at[2, 0])
    load2 = pltpu.make_async_copy(w2, W2, loc.at[2, 1])

    barrier = pltpu.get_barrier_semaphore()

    def greet(where):
        pl.semaphore_signal(barrier, inc=1, device_id=where, device_id_type=MESH)

    for where in (sib, dev(ox, z, c), dev(ox, z, oc), partner, crossed, dev(ox, zc, c)):
        greet(where)

    def greet_peer(i, _):
        k = (me + i) % PEERS
        greet(dev(k % 2, z, c, k // 2))
        return 0

    lax.fori_loop(1, PEERS, greet_peer, 0)

    @pl.when(s < SECTIONS - 1)
    def _():
        greet(dev(xl, z, 0, s + 1))
        greet(dev(xl, z, 1, s + 1))

    @pl.when(s == SECTIONS - 1)
    def _():
        def greet_source(i, _):
            k = i * 2 + xl

            @pl.when(jnp.logical_not((k == me) & (c == 0)))
            def _():
                greet(dev(k % 2, z, 0, k // 2))

            greet(dev(k % 2, zi, 1, k // 2))
            return 0

        lax.fori_loop(0, PEERS // 2, greet_source, 0)

    zt = z + c * (zi - z)
    xt, ct, sub = xl, s // 4, s % 4
    own_final = (s == SECTIONS - 1) & (xt == xl) & (zt == z)

    def lane_cols(x, cc):
        return at((x * 2 + cc) * QUARTER, QUARTER)

    def piece_rows(x, cc, half):
        return at((x * 2 + cc) * TOK + half * PART, PART)

    def kv_piece(i, r, half):
        source, held = ((kvg, GA), (kvw, GB))[i]
        x, cc = lanes[r]
        part = source.at[pl.ds(half * PART, PART), lane_cols(x, cc)]
        target = held.at[0, piece_rows(xl, c, half)]
        if r == 0:
            return pltpu.make_async_copy(part, target, loc.at[i, half])
        return rc(part, target, kv_s.at[i, r, half], kv_r.at[i, r, half], dev(x, z, cc))

    def z_piece(i, r, half):
        held, where = (GA, partner) if i == 0 else (GB, crossed)
        rows = piece_rows(*lanes[r], half)
        if r == 0:
            source = (kvg, kvw)[i].at[pl.ds(half * PART, PART), lane_cols(xl, c)]
        else:
            source = held.at[0, rows]
        return rc(source, held.at[1, rows], zk_s.at[i, r, half], zk_r.at[i, r, half], where)

    pl.semaphore_wait(
        barrier, 6 + PEERS - 1 + 2 * (s > 0).astype(jnp.int32) + 2 - own_final.astype(jnp.int32)
    )
    for i in range(2):
        for half in range(2):
            for r in (2, 3):
                go(kv_piece(i, r, half), ("kv", i, r, half))
    for i in range(2):
        for half in range(2):
            go(kv_piece(i, 1, half), ("kv", i, 1, half))
            go(z_piece(i, 0, half), ("zk", i, 0, half))
    for i in range(2):
        for half in range(2):
            kv_piece(i, 0, half).start()
    load1.start()
    load2.start()

    def norm_rows(j, _):
        rows = at(j * 32, 32)
        values = enc[rows, :].astype(F32)
        factor = lax.rsqrt(jnp.mean(values * values, axis=1, keepdims=True) + EPSILON)
        NB[rows, :] = (values * factor * gain[...]).astype(BF)
        return 0

    lax.fori_loop(0, TOK // 32, norm_rows, 0)
    zh = z // 2
    xd = (ids[...] // 2 != xl).astype(jnp.int32)
    zd = (ids[...] % 2 != zh).astype(jnp.int32)
    block = xd + 2 * zd
    which = lax.broadcasted_iota(jnp.int32, (16, TOK), 0)
    first, second = block[0:1, :] == which, block[1:2, :] == which
    used = (first | second).astype(F32)
    weight = jnp.where(first, probs[0:1, :], 0.0) + jnp.where(second, probs[1:2, :], 0.0)
    row, col = (lax.broadcasted_iota(jnp.int32, (TOK, TOK), i) for i in range(2))
    ahead = dot_nn(used.astype(BF), (row < col).astype(BF)) + (c * CAP).astype(F32)
    rest = jnp.zeros((TOK - 16, TOK), F32)
    ahead_t = jnp.concatenate([ahead, rest], axis=0).T
    used_t = jnp.concatenate([used, rest], axis=0).T
    slot = lax.broadcasted_iota(jnp.int32, (BLOCK, TOK), 0).astype(F32)
    column = lax.broadcasted_iota(jnp.int32, (TOK, STEP), 1).astype(F32)
    for p in range(EXPERTS):
        WX[c, rows_of(p), :] = jnp.where(slot == ahead[p:p + 1, :], weight[p:p + 1, :], 0.0)
        hit = jnp.where(column == ahead_t[:, p:p + 1], used_t[:, p:p + 1], 0.0)
        STX[c, :, pl.ds(p * STEP, STEP)] = hit.astype(BF)

    exchange = [
        rc(NB.at[:, their_cols], TK.at[my_toks], ex_s.at[0], ex_r.at[0], sib),
        rc(WX.at[c], WX.at[c], ex_s.at[1], ex_r.at[1], sib),
        rc(STX.at[c], STX.at[c], ex_s.at[2], ex_r.at[2], sib),
    ]
    for i in range(3):
        go(exchange[i], ("ex", i))
    TK[my_toks, :] = NB[:, my_cols]

    def kv_forward(i, r, half):
        got(("kv", i, r, half))
        go(z_piece(i, r, half), ("zk", i, r, half))

    for i in range(2):
        for half in range(2):
            kv_forward(i, 1, half)
    for r in (2, 3):
        kv_forward(0, r, 0)

    for i in range(3):
        got(("ex", i))

    def weights_of(p):
        both = jnp.concatenate([WX[0, rows_of(p), :], WX[1, rows_of(p), :]], axis=1)
        return both, (both > 0).astype(BF)

    for p in range(EXPERTS):
        _, hot = weights_of(p)
        slots = dot_nn(hot, TK[...]).astype(BF)
        if p == OWN:
            XN[0, c, rows_of(p)] = slots
        else:
            LN[p] = slots

    def stage1(a, p):
        source, held = ((LN, XN), (LS, XS))[a]
        return rc(source.at[p], held.at[0, c, rows_of(p)], st_s.at[a, p], st_r.at[a, p], group[p])

    def to_partner(a, p):
        held = (XN, XS)[a]
        return rc(held.at[0, c, rows_of(p)], held.at[1, c, rows_of(p)], pa_s.at[a, p], pa_r.at[a, p], partner)

    def to_sib(a, h, p):
        part = (XN, XS)[a].at[h, c, rows_of(p)]
        return rc(part, part, sb_s.at[a, h, p], sb_r.at[a, h, p], sib)

    def send_out(a, p):
        copy = stage1(a, p)
        go(copy, ("st", a, p))
        return copy

    def pass_on(a, p):
        go(to_partner(a, p), ("pa", a, p))
        go(to_sib(a, 0, p), ("sb", a, 0, p))

    def forward(a, p):
        got(("st", a, p))
        pass_on(a, p)

    def hand_over(a, p):
        got(("pa", a, p))
        go(to_sib(a, 1, p), ("sb", a, 1, p))

    def take(a, h, blocks):
        for p in blocks:
            part = (XN, XS)[a].at[h, oc, rows_of(p)]
            got(("sb", a, h, p), rc(part, part, sb_s.at[a, h, p], sb_r.at[a, h, p], sib))

    send_out(0, 1)
    send_out(0, 2)
    for r in (2, 3):
        kv_forward(0, r, 1)
    pass_on(0, OWN)
    for r in (2, 3):
        kv_forward(1, r, 0)
    forward(0, 2)
    for r in (2, 3):
        kv_forward(1, r, 1)

    def pend_copy(core):
        return rc(pend.at[:, pl.ds(core * HALF, HALF)], INC.at[my_toks], pe_s.at[core], inc_r, dev(xl, z, core, s - 1))

    for i in range(2):
        for half in range(2):
            kv_piece(i, 0, half).wait()
            for r in range(LANES):
                if i == 0:
                    got(("zk", 0, r, half))

    def product(plane, p, store):
        for j in range(2):
            cols = pl.ds(j * STEP, STEP)
            store(p, cols, dot_nt(GA[plane], GB[p, cols, :]))

    def keep_theirs(p, cols, value):
        QS[p, :, cols] = value.astype(BF)

    def keep_mine(p, cols, value):
        PF[p, :, cols] = value

    def chunk_of(k):
        return at((k % 2 * 8 + k // 2) * CHUNK, CHUNK)

    def share(p, k):
        return rc(QO.at[p, chunk_of(k)], RS.at[p, me], rs_s.at[p, k], rs_r.at[p, me], dev(k % 2, z, c, k // 2))

    def share_in(p, k):
        return rc(RS.at[p, k], RS.at[p, k], rs_s.at[p, k], rs_r.at[p, k], dev(k % 2, z, c, k // 2))

    def spread(p):
        got(("swap", p))

        def add_core(j, _):
            rows = at(j * 64, 64)
            QO[p, rows, :] = (PF[p, rows, :] + QR[p, rows, :].astype(F32)).astype(BF)
            return 0

        lax.fori_loop(0, PLANE // 64, add_core, 0)

        def send_share(i, _):
            share(p, (me + i) % PEERS).start()
            return 0

        lax.fori_loop(1, PEERS, send_share, 0)
        RS[p, me] = QO[p, chunk_of(me), :]

    def half_product(p):
        product(oc, p, keep_theirs)
        go(rc(QS.at[p], QR.at[p], q_s.at[p], q_r.at[p], sib), ("swap", p))
        product(c, p, keep_mine)

    send_out(0, 3)
    half_product(0)
    spread(0)
    forward(0, 1)
    for half in range(2):
        for r in range(LANES):
            got(("zk", 1, r, half))
    half_product(1)
    spread(1)

    @pl.when(s > 0)
    def _():
        pend_copy(0).start()
        pend_copy(1).start()

    def pre_act(h, first, rows):
        span = pl.ds(first, rows)

        def tile(j, _):
            cols = at(j * WIDE, WIDE)
            total = dot_nn(XN[h, 0, span], W1[pl.ds(0, HALF), cols]) + dot_nn(XN[h, 1, span], W1[pl.ds(HALF, HALF), cols])
            GP[h, span, cols] = gelu_slope(total).astype(BF)
            return 0

        lax.fori_loop(0, D // WIDE, tile, 0)

    load1.wait()

    def settle(p):
        def wait_share(i, _):
            share_in(p, (me + i) % PEERS).wait_recv()
            return 0

        lax.fori_loop(1, PEERS, wait_share, 0)
        total = RS[p, 0].astype(F32)
        for k in range(1, PEERS):
            total = total + RS[p, k].astype(F32)
        FIN[p] = total.astype(BF)
        for x in range(2):
            final(p, x, "start")

    def final(p, x, op):
        zz = z if p == 0 else zc
        source = FIN.at[p, :, pl.ds(x * STEP, STEP)]
        target = INC.at[at(ct * TOK + sub * CHUNK, CHUNK), at(zz * STEP, STEP)]
        away = rc(source, target, fi_s.at[p, x], inc_r, dev(xt, zt, x, SECTIONS - 1))
        at_home = jnp.logical_and(own_final, c == x)

        @pl.when(jnp.logical_not(at_home))
        def _():
            away.start() if op == "start" else away.wait_send()

        if op == "start":
            @pl.when(at_home)
            def _():
                pltpu.make_async_copy(source, target, inc_r).start()

    settle(0)
    forward(0, 3)
    take(0, 0, (0, 1))
    pre_act(0, 0, PAIR)
    hand_over(0, 0)
    hand_over(0, 2)
    take(0, 0, (2, 3))
    pre_act(0, PAIR, PAIR)
    settle(1)
    hand_over(0, 1)
    take(0, 1, (0, 1))
    pre_act(1, 0, PAIR)
    hand_over(0, 3)
    take(0, 1, (2, 3))
    pre_act(1, PAIR, PAIR)
    pltpu.make_async_copy(INC, INC, inc_r).wait()

    def scaled(p):
        both, hot = weights_of(p)
        return (dot_nn(hot, INC[...]) * jnp.sum(both, axis=1, keepdims=True)).astype(BF)

    XS[0, c, rows_of(OWN)] = scaled(OWN)
    pass_on(1, OWN)
    LS[1] = scaled(1)
    leaving = send_out(1, 1)
    LS[2] = scaled(2)
    send_out(1, 2)
    LS[3] = scaled(3)
    go(rc(INC.at[their_toks], INCX, ix_s, ix_r, sib), "inc")
    gone(leaving)
    send_out(1, 3)
    forward(1, 1)
    forward(1, 2)
    hand_over(1, 0)
    load2.wait()

    def hidden(h, first, rows):
        span = pl.ds(first, rows)

        def tile(j, _):
            cols = at(j * WIDE, WIDE)
            upstream = dot_nt(XS[h, 0, span], W2[cols, pl.ds(0, HALF)]) + dot_nt(XS[h, 1, span], W2[cols, pl.ds(HALF, HALF)])
            GP[h, span, cols] = (upstream * GP[h, span, cols].astype(F32)).astype(BF)
            return 0

        lax.fori_loop(0, D // WIDE, tile, 0)

    def pieces(h, first, rows):
        span = pl.ds(first, rows)
        for core, kept in ((oc, SB), (c, PH)):
            def tile(j, _, core=core, kept=kept):
                cols = at(j * WIDE, WIDE)
                kept[h, span, cols] = dot_nt(GP[h, span, :], W1[at(core * HALF + j * WIDE, WIDE), :]).astype(BF)
                return 0

            lax.fori_loop(0, HALF // WIDE, tile, 0)
            if kept is SB:
                i = 2 * h + first // PAIR
                go(rc(SB.at[h, span], SR.at[h, span], ss_s.at[i], ss_r.at[i], sib), ("ss", i))

    def partner_sum(p):
        return rc(PS.at[rows_of(p)], PR.at[rows_of(p)], ps_s.at[p], ps_r.at[p], partner)

    def add_cores(i, blocks):
        got(("ss", 2 + i))
        for p in blocks:
            def some(j, _, p=p):
                rows = at(p * BLOCK + j * 48, 48, 16)
                PS[rows, :] = (PH[1, rows, :].astype(F32) + SR[1, rows, :].astype(F32)).astype(BF)
                return 0

            lax.fori_loop(0, 3, some, 0)
            go(partner_sum(p), ("ps", p))

    take(1, 0, (0, 1))
    hidden(0, 0, PAIR)
    forward(1, 3)
    pieces(0, 0, PAIR)
    hand_over(1, 1)
    take(1, 1, (0, 1))
    hidden(1, 0, PAIR)
    hand_over(1, 2)
    pieces(1, 0, PAIR)
    add_cores(0, (1, 0))
    take(1, 0, (2, 3))
    hidden(0, PAIR, PAIR)
    hand_over(1, 3)
    pieces(0, PAIR, PAIR)
    take(1, 1, (2, 3))
    hidden(1, PAIR, PAIR)

    def complete(p):
        got(("ps", p))
        held = CR if p == OWN else CS

        def some(j, _):
            rows = at(p * BLOCK + j * 48, 48, 16)
            value = PH[0, rows, :].astype(F32) + SR[0, rows, :].astype(F32) + PR[rows, :].astype(F32)
            held[p, at(j * 48, 48, 16), :] = value.astype(BF)
            return 0

        lax.fori_loop(0, 3, some, 0)
        if p != OWN:
            go(rc(CS.at[p], CR.at[p], cr_s.at[p], cr_r.at[p], group[p]), ("cr", p))

    def gathered(core, p):
        return dot_nn(STX[core, :, pl.ds(p * STEP, BLOCK)], CR[p])

    got(("ss", 0))
    complete(1)
    pieces(1, PAIR, PAIR)
    add_cores(1, (3, 2))
    complete(OWN)
    got(("ss", 1))
    complete(3)
    got(("cr", 1))
    NS[...] = gathered(oc, OWN) + gathered(oc, 1)
    NG[...] = gathered(c, OWN) + gathered(c, 1)
    complete(2)
    got(("cr", 3))
    NS[...] = NS[...] + gathered(oc, 3)
    NG[...] = NG[...] + gathered(c, 3)
    got(("cr", 2))
    NS[...] = NS[...] + gathered(oc, 2)
    go(rc(NS, NR, n_s, n_r, sib), "last")
    NG[...] = NG[...] + gathered(c, 2)
    got("inc")
    got("last")

    def finish(j, _):
        rows = at(j * 32, 32)
        mine_x, their_x = enc[rows, my_cols].astype(F32), enc[rows, their_cols].astype(F32)
        mine_g, their_g = NG[rows, :] * gain[:, my_cols], NR[rows, :] * gain[:, their_cols]
        power = jnp.sum(mine_x * mine_x, axis=1, keepdims=True) + jnp.sum(their_x * their_x, axis=1, keepdims=True)
        factor = lax.rsqrt(power * (1.0 / D) + EPSILON)
        along = jnp.sum(mine_g * mine_x, axis=1, keepdims=True) + jnp.sum(their_g * their_x, axis=1, keepdims=True)
        pull = along * factor * factor * factor * (1.0 / D)
        incoming = INC[at(c * TOK + j * 32, 32), :].astype(F32)
        out[rows, my_cols] = (incoming + mine_g * factor - mine_x * pull).astype(BF)
        out[rows, their_cols] = (INCX[rows, :].astype(F32) + their_g * factor - their_x * pull).astype(BF)
        return 0

    lax.fori_loop(0, TOK // 32, finish, 0)

    @pl.when(s > 0)
    def _():
        pend_copy(0).wait_send()
        pend_copy(1).wait_send()

    def sent_share(i, _):
        for p in range(2):
            share(p, (me + i) % PEERS).wait_send()
        return 0

    lax.fori_loop(1, PEERS, sent_share, 0)
    for p in range(2):
        for x in range(2):
            final(p, x, "wait")
    for copy in sent:
        copy.wait_send()


def tick(kvg, kvw, pend, enc, gain, ids, probs, w1, w2):
    any_place = pl.BlockSpec(memory_space=pl.ANY)
    vmem = pl.BlockSpec(memory_space=pltpu.VMEM)
    dma = pltpu.SemaphoreType.DMA
    V = pltpu.VMEM
    scratch = [
        V((D, D), BF), V((D, D), BF),
        V((2, PLANE, QUARTER), BF), V((2, PLANE, QUARTER), BF),
        V((2, PLANE, PLANE), BF), V((2, PLANE, PLANE), BF), V((2, PLANE, PLANE), BF), V((2, PLANE, PLANE), F32),
        V((2, PEERS, CHUNK, PLANE), BF), V((2, CHUNK, PLANE), BF),
        V((2 * TOK, HALF), BF), V((TOK, HALF), BF), V((TOK, D), BF), V((2 * TOK, HALF), BF),
        V((2, SIDE, TOK), F32), V((2, TOK, EXPERTS * STEP), BF),
        V((EXPERTS, BLOCK, HALF), BF), V((EXPERTS, BLOCK, HALF), BF),
        V((2, 2, SIDE, HALF), BF), V((2, 2, SIDE, HALF), BF),
        V((2, SIDE, D), BF),
        V((2, SIDE, HALF), BF), V((2, SIDE, HALF), BF), V((2, SIDE, HALF), BF),
        V((SIDE, HALF), BF), V((SIDE, HALF), BF),
        V((EXPERTS, BLOCK, HALF), BF), V((EXPERTS, BLOCK, HALF), BF),
        V((TOK, HALF), F32), V((TOK, HALF), F32), V((TOK, HALF), F32),
        dma((3, 2)), dma((3,)), dma((3,)), dma((2,)), dma, dma((2, 4, 2)), dma((2, 4, 2)), dma((2, 4, 2)), dma((2, 4, 2)),
        dma((2,)), dma((2,)), dma((2, PEERS)), dma((2, PEERS)), dma((2, 2)), dma, dma,
        dma((2, 4)), dma((2, 4)), dma((2, 4)), dma((2, 4)), dma((2, 2, 4)), dma((2, 2, 4)),
        dma((4,)), dma((4,)), dma((4,)), dma((4,)), dma((4,)), dma((4,)), dma, dma,
    ]
    return pl.pallas_call(
        tick_kernel,
        out_shape=jax.ShapeDtypeStruct((TOK, D), BF),
        in_specs=[any_place] * 3 + [vmem] * 4 + [any_place] * 2,
        out_specs=vmem,
        scratch_shapes=scratch,
        compiler_params=pltpu.CompilerParams(
            collective_id=0, has_side_effects=True, vmem_limit_bytes=62 * 1024 * 1024
        ),
        name="tick",
    )(kvg, kvw, pend, enc, gain, ids, probs, w1, w2)


def body(
    kv_grads, kv_weight, enc_inputs, enc_gain, enc_w1, enc_w2, route_ids, route_probs, pending_grads
):
    return tick(
        kv_grads[0], kv_weight[0], pending_grads[0], enc_inputs[0], enc_gain, route_ids[0].T, route_probs[0].T,
        enc_w1[0], enc_w2[0],
    )[None]


def solution(mesh):
    return jax.shard_map(
        body,
        mesh=mesh,
        in_specs=(
            P("section", "expert", None),
            P("section", "expert", None),
            P("section", "expert", None),
            P("section", None),
            P("section", None, "expert"),
            P("section", "expert", None),
            P("section", "expert", None),
            P("section", "expert", None),
            P("section", "expert", None),
        ),
        out_specs=P("section", "expert", None),
        check_vma=False,
    )
```
